128 devices in a mesh: layer: 8 (over x, z_hi), feat: 16 (over z_lo, y, core).
Axes of the slice: x: 4, y: 4, z: 4 (z_hi: 2, z_lo: 2; z = z_hi * 2 + z_lo), core: 2. Of those that a mesh axis runs over, the one named last changes fastest.
Arguments:
- sources: bfloat16 [2, 384, 4608], P(None, 'feat'), may hold values from -6 to 6
- targets: bfloat16 [4, 384, 4608], P(None, 'feat'), may hold values from -6 to 6
- blocks: bfloat16 [8, 32768, 4608], P('layer', 'feat'), may hold values from -0.09375 to 0.09375
- enc_bias: float32 [2, 32768], P(None, 'feat'), may hold values from -4 to 4
- token_code: int32 [2, 384], replicated, may hold values from 1 to 250
- feature_threshold_code: int32 [2, 32768], P(None, 'feat'), may hold values from 1 to 250
- dec_map: int32 [6], replicated, may hold values from 0 to 5, each once
Outputs:
- recon_error: float32 [4, 384, 4608], P(None, 'feat')
- pre_grads: bfloat16 [2, 384, 32768], P(None, 'layer', 'feat')
The draws below stay inside these ranges and needn't reach their ends.
Inputs may be any that keep to these rules, and one draw needn't show every extreme that they name: `dec_map`: each pair number 0 to 5 stands once.
All inputs are finite; a program needn't handle non-finite values.
Results may differ from the reference program's by a relative error of at most 0.02.
Values may be sent and summed in bfloat16 or wider, within the bound.
A program may use at most 128 MiB of HBM per device.

```python
import jax
import jax.numpy as jnp

D = 4608
F = 32768
K = 3
TOK = 384
S = 2
NT = 4
BLOCKS = 8
N_FEAT = 16


def set_ends(values, rng, low, top_value):
    longest = values.shape.index(max(values.shape))
    spots = []
    for shift in (0, 1):
        where = [jax.random.randint(jax.random.fold_in(rng, axis), (), 0, length) for axis, length in enumerate(values.shape)]
        where[longest] = (where[longest] + shift) % values.shape[longest]
        spots.append(tuple(where))
    return values.at[spots[0]].set(low).at[spots[1]].set(top_value)


def steps_of(stream_key, extent, shards, low, high):
    factor_of, own = 1.0, jax.random.fold_in(stream_key, 6)
    for axis_at, shards_of in shards:
        heights = jnp.exp(jax.random.uniform(jax.random.fold_in(own, axis_at), (shards_of,), jnp.float32, low / len(shards), high / len(shards)))
        factor_of = factor_of * jnp.repeat(heights, extent[axis_at] // shards_of).reshape([-1 if axis == axis_at else 1 for axis in range(len(extent))])
    return factor_of


def gaussian(key, extent, width, most, cuts=(), kind=jnp.bfloat16):
    values = width * jax.random.normal(key, extent, jnp.float32)
    if cuts:
        values = values * steps_of(key, extent, cuts, -0.22, 0.18)
    return jnp.clip(values, -most, most).astype(kind)


def setup_inputs(seed: int = 0) -> dict:
    streams_of = jax.random.split(jax.random.key(seed), 8)
    return {
        "sources": gaussian(streams_of[0], (S, TOK, D), 1.0, 6.0, ((1, 16),)),
        "targets": gaussian(streams_of[1], (NT, TOK, D), 1.0, 6.0, ((1, 16),)),
        "blocks": gaussian(streams_of[2], (BLOCKS, F, D), D ** -0.5, 0.09375, ((0, 8), (1, 16))),
        "enc_bias": gaussian(streams_of[3], (S, F), 1.0, 4.0, ((1, 16),), jnp.float32),
        "token_code": set_ends(jax.random.randint(streams_of[4], (S, TOK), 1, 251), jax.random.fold_in(streams_of[4], 1), 1, 250).astype(jnp.int32),
        "feature_threshold_code": set_ends(jax.random.randint(streams_of[5], (S, F), 1, 251), jax.random.fold_in(streams_of[5], 1), 1, 250).astype(jnp.int32),
        "dec_map": jax.random.permutation(streams_of[6], S * K).astype(jnp.int32),
    }


def reference(sources, targets, blocks, enc_bias, token_code, feature_threshold_code, dec_map):
    sources_n = sources.shape[0]
    gates = (((token_code[:, :, None] * feature_threshold_code[:, None, :]) % 251) < 40).astype(jnp.float32)
    feats = []
    for source in range(sources_n):
        pre = jnp.dot(sources[source], blocks[source].T, preferred_element_type=jnp.float32) + enc_bias[source]
        feats.append((pre * gates[source]).astype(jnp.bfloat16))
    feats = jnp.stack(feats)
    pairs = dec_map.astype(jnp.int32)
    shard_width = F // N_FEAT
    recon = jnp.zeros(targets.shape, jnp.float32)
    for index in range(sources_n * K):
        anchor = pairs[index] // K
        target = anchor + pairs[index] % K
        term = jnp.zeros((targets.shape[1], targets.shape[2]), jnp.float32)
        for shard in range(N_FEAT):
            lower = shard * shard_width
            upper = lower + shard_width
            partial_value = jnp.dot(feats[anchor][:, lower:upper], blocks[sources_n + index][lower:upper],
                              preferred_element_type=jnp.float32)
            term = term + partial_value.astype(jnp.bfloat16).astype(jnp.float32)
        recon = recon.at[target].add(term)
    recon_error = recon - targets.astype(jnp.float32)
    error_low = recon_error.astype(jnp.bfloat16)
    grads = jnp.zeros((sources_n, TOK, F), jnp.float32)
    for index in range(sources_n * K):
        anchor = pairs[index] // K
        target = anchor + pairs[index] % K
        term = jnp.dot(error_low[target], blocks[sources_n + index].T, preferred_element_type=jnp.float32)
        grads = grads.at[anchor].add(term)
    return recon_error, (grads * gates).astype(jnp.bfloat16)
```

```python
import jax
import jax.numpy as jnp
from jax import lax
from jax.experimental import pallas as pl
from jax.experimental.pallas import tpu as pltpu
from jax.sharding import PartitionSpec as P

MESH = pl.DeviceIdType.MESH
F32 = jnp.float32
BF16 = jnp.bfloat16

ROWS = 48
HALF = 2304
WIDE = (1024, 1280)
COL = (0, 1024)
NCH = 8
CH = 256
HR = 192
CROSS0 = 3
FLAG = 3
LH = 1
ML = 6
GN = 4
GC = 512

NT = (((1,), (1,)), ((), ()))
PAIRS = ((0,), (1, 3), (2, 4), (5,))


def gate_of(tok, code):
    v = tok * code
    q = jnp.floor(v * (1.0 / 251.0))
    return (v - 251.0 * q) < 40.0


def kernel(
    dm, src, tgt, w_hbm, bias, tok, fc, err_out, pg_out,
    W, X0, X1, FB, acc, sx_send, sx, tg_send, tg, TK, FC,
    S0, S1, C0, C1, T0, T1, RZ0, RY1, V0, RY0, V1, RZ1, RL0, RL1, E0, E1, ER0, ER1, GS, GR,
    wsem, xsem, ags, agr, bs, br, fs, fcs, fr, cs, cr, ls, lr, es, er, gs, gr,
):
    layer = lax.axis_index("layer")
    feat = lax.axis_index("feat")
    x, h = layer // 2, layer % 2
    l, y, c = feat // 8, (feat // 2) % 4, feat % 2
    u = feat // 2
    o = 1 - c
    uz = (1 - l) * 4 + y
    X = (X0, X1)

    def dev(x=x, h=h, l=l, y=y, c=c):
        return (2 * x + h, (4 * l + y) * 2 + c)

    ys = [lax.rem(y + k, 4) for k in (1, 2, 3)]
    xs = [lax.rem(x + k, 4) for k in (1, 2, 3)]
    sib = dev(c=o)
    zp = dev(l=1 - l)
    cross = dev(h=1 - h)

    bar = pltpu.get_barrier_semaphore()
    peers = [sib, zp, cross]
    peers += [dev(y=a) for a in ys] + [dev(y=a, l=1 - l) for a in ys]
    peers += [dev(x=a) for a in xs] + [dev(x=a, h=1 - h) for a in xs]
    for p in peers:
        pl.semaphore_signal(bar, inc=1, device_id=p, device_id_type=MESH)

    wcp = [
        pltpu.make_async_copy(w_hbm.at[0, pl.ds(CH * k, CH)], W.at[pl.ds(CH * k, CH)], wsem.at[k])
        for k in range(NCH)
    ]
    for cp in wcp:
        cp.start()

    for s in range(2):
        TK[s] = jnp.transpose(jnp.broadcast_to(tok[s : s + 1, :].astype(F32), (128, 384)))
    FC[...] = fc[...].astype(F32)

    def rcopy(a, b, ssem, rsem, to, sends):
        cp = pltpu.make_async_remote_copy(
            src_ref=a, dst_ref=b, send_sem=ssem, recv_sem=rsem, device_id=to, device_id_type=MESH
        )
        cp.start()
        sends.append(cp)

    def arrived(b, rsem):
        pltpu.make_async_remote_copy(
            src_ref=b, dst_ref=b, send_sem=rsem, recv_sem=rsem, device_id=sib, device_id_type=MESH
        ).wait_recv()

    pl.semaphore_wait(bar, len(peers))

    def half_of(v, which):
        return jnp.where(which == 0, v[..., :HALF], v[..., HALF:])

    first = []
    own = pl.ds(pl.multiple_of(24 * c, 8), 24)
    for t in range(4):
        v = tgt[t].astype(F32)
        tg_send[t] = half_of(v, o)
        tg[t, own, :] = half_of(v, c)
    v = jnp.where(h == 0, src[0].astype(F32), src[1].astype(F32))
    sx_send[...] = half_of(v, o)
    sx[own, :] = half_of(v, c)
    rcopy(sx_send, sx.at[own, :], xsem.at[0], xsem.at[1], sib, first)
    rcopy(tg_send, tg.at[:, own, :], xsem.at[2], xsem.at[3], sib, first)
    other = pl.ds(pl.multiple_of(24 * o, 8), 24)
    arrived(sx.at[other, :], xsem.at[1])
    arrived(tg.at[:, other, :], xsem.at[3])
    for cp in first:
        cp.wait_send()

    def all_gather():
        sends = []
        n = [0]

        def send(p, b, to, rsem=None):
            r = X[p].at[c, b]
            rcopy(r, r, ags.at[n[0]], agr.at[p, b] if rsem is None else rsem, to, sends)
            n[0] += 1

        def both(p, b):
            send(p, b, sib, br.at[p, b])

        send(0, u, zp)
        for k in range(3):
            send(1, u, dev(y=ys[k]))
            send(0, u, dev(y=ys[k]))
        send(1, u, zp)
        both(0, u)
        both(1, u)
        arrived(X0.at[c, uz], agr.at[0, uz])
        for k in range(3):
            send(0, uz, dev(y=ys[k]))
        both(0, uz)
        for k in (0, 2, 1):
            b = l * 4 + ys[k]
            arrived(X1.at[c, b], agr.at[1, b])
            send(1, b, zp)
            both(1, b)
        for k in (0, 2, 1):
            b = l * 4 + ys[k]
            arrived(X0.at[c, b], agr.at[0, b])
            both(0, b)
        arrived(X1.at[c, uz], agr.at[1, uz])
        both(1, uz)
        for k in (0, 2, 1):
            b = (1 - l) * 4 + ys[k]
            arrived(X0.at[c, b], agr.at[0, b])
            both(0, b)
            arrived(X1.at[c, b], agr.at[1, b])
            both(1, b)
        for p in range(2):
            for b in range(8):
                arrived(X[p].at[o, b], br.at[p, b])
        for cp in sends:
            cp.wait_send()

    def against(rows):
        total = None
        for cc in range(2):
            for p in range(2):
                a = X[p][cc].reshape(384, WIDE[p])
                b = W[rows, cc * HALF + COL[p] : cc * HALF + COL[p] + WIDE[p]]
                d = lax.dot_general(a, b, NT, preferred_element_type=F32)
                total = d if total is None else total + d
        return total

    @pl.when(x == 0)
    def _():
        for p in range(2):
            X[p][c, u] = sx[:, COL[p] : COL[p] + WIDE[p]].astype(BF16)
        all_gather()
        line = (dev(x=1), dev(x=3))

        def chunk(k, _):
            rows = pl.ds(pl.multiple_of(k * CH, CH), CH)
            pltpu.make_async_copy(w_hbm.at[0, rows], W.at[rows], wsem.at[k]).wait()
            pre = against(rows) + bias[pl.ds(h, 1), rows]
            on = gate_of(jnp.concatenate([TK[h]] * 2, axis=1), FC[pl.ds(h, 1), rows])
            FB[h, k] = jnp.where(on, pre, 0.0).astype(BF16).reshape(2, HR, CH)
            junk = []
            for half in range(2):
                r = FB.at[h, k, half]
                rcopy(r, r, fs.at[h, k, half], fr.at[h, k, half], line[half], junk)

            @pl.when(k < CROSS0)
            def _():
                for half in range(2):
                    r = FB.at[h, k, half]
                    rcopy(r, r, fcs.at[k, half], fr.at[h, k, half], cross, junk)

            j = k - FLAG

            @pl.when((j >= 0) & (j < CROSS0))
            def _():
                for half in range(2):
                    r = FB.at[1 - h, j, half]
                    arrived(r, fr.at[1 - h, j, half])
                    rcopy(r, r, fs.at[1 - h, j, half], fr.at[1 - h, j, half], line[half], junk)

            return 0

        lax.fori_loop(0, NCH, chunk, 0)

        def drain(k, _):
            for half in range(2):
                r = FB.at[h, k, half]
                pltpu.make_async_remote_copy(r, r, fs.at[h, k, half], fr.at[h, k, half], line[half], MESH).wait_send()

                @pl.when(k < CROSS0)
                def _():
                    pltpu.make_async_remote_copy(r, r, fcs.at[k, half], fr.at[h, k, half], cross, MESH).wait_send()
                    q = FB.at[1 - h, k, half]
                    pltpu.make_async_remote_copy(q, q, fs.at[1 - h, k, half], fr.at[1 - h, k, half], line[half], MESH).wait_send()

            return 0

        lax.fori_loop(0, NCH, drain, 0)

    slot = jnp.maximum(layer - 2, 0)
    pair = dm[slot]
    mine_src = (pair >= 3).astype(jnp.int32)
    mine_tgt = pair - 2 * mine_src
    place = []
    for p in range(6):
        at = jnp.int32(0)
        for i in range(6):
            at = jnp.where(dm[i] == p, jnp.int32(i + 2), at)
        place.append(at)

    @pl.when(x > 0)
    def _():
        acc[...] = jnp.zeros_like(acc)
        nxt = (dev(x=lax.rem(x + 1, 4)), dev(x=lax.rem(x + 3, 4)))
        more = (x < 3, x > 1)
        lag = ((x - 1) * LH, (3 - x) * LH)

        def fwd(s, k, half):
            r = FB.at[s, k, half]
            return pltpu.make_async_remote_copy(r, r, fs.at[s, k, half], fr.at[s, k, half], nxt[half], MESH)

        def over(k, half):
            r = FB.at[h, k, half]
            return pltpu.make_async_remote_copy(r, r, fcs.at[k, half], fr.at[h, k, half], cross, MESH)

        def step(t, _):
            for half in range(2):
                k = t - lag[half]

                @pl.when((k >= 0) & (k < NCH))
                def _():
                    arrived(FB.at[h, k, half], fr.at[h, k, half])

                    @pl.when(more[half])
                    def _():
                        fwd(h, k, half).start()

                    @pl.when(k >= CROSS0)
                    def _():
                        over(k, half).start()

                j = k - FLAG

                @pl.when((j >= 0) & (j < CROSS0))
                def _():
                    arrived(FB.at[1 - h, j, half], fr.at[1 - h, j, half])

                    @pl.when(more[half])
                    def _():
                        fwd(1 - h, j, half).start()

            m = t - ML

            @pl.when((m >= 0) & (m < NCH))
            def _():
                @pl.when(m >= CROSS0)
                def _():
                    for half in range(2):
                        arrived(FB.at[1 - h, m, half], fr.at[1 - h, m, half])

                rows = pl.ds(pl.multiple_of(m * CH, CH), CH)
                pltpu.make_async_copy(w_hbm.at[0, rows], W.at[rows], wsem.at[m]).wait()
                a = jnp.where(mine_src == 0, FB[0, m], FB[1, m]).reshape(384, CH)
                for cc in range(2):
                    for n in range(3):
                        cols = slice(cc * HALF + n * 768, cc * HALF + (n + 1) * 768)
                        acc[cc, :, n * 768 : (n + 1) * 768] += jnp.dot(a, W[rows, cols], preferred_element_type=F32)

            return 0

        lax.fori_loop(0, NCH + ML, step, 0)

        def drain(k, _):
            for half in range(2):

                @pl.when(more[half])
                def _():
                    fwd(h, k, half).wait_send()

                    @pl.when(k < CROSS0)
                    def _():
                        fwd(1 - h, k, half).wait_send()

                @pl.when(k >= CROSS0)
                def _():
                    over(k, half).wait_send()

            return 0

        lax.fori_loop(0, NCH, drain, 0)

        sends = []
        S, C, T = (S0, S1), (C0, C1), (T0, T1)
        for p in range(2):
            cols = slice(COL[p], COL[p] + WIDE[p])
            S[p][...] = acc[o, :, cols].astype(BF16).reshape(8, ROWS, WIDE[p])
            rcopy(S[p], C[p], cs.at[p], cr.at[p], sib, sends)
        for p in range(2):
            cols = slice(COL[p], COL[p] + WIDE[p])
            arrived(C[p], cr.at[p])
            T[p][...] = (acc[c, :, cols] + C[p][...].astype(F32).reshape(384, WIDE[p])).astype(BF16).reshape(8, ROWS, WIDE[p])
            if p == 0:
                rcopy(T0.at[pl.ds((1 - l) * 4, 4)], RZ0, cs.at[2], cr.at[2], zp, sends)
        for k in range(3):
            for q in range(2):
                rcopy(T1.at[q * 4 + ys[k]], RY1.at[2 - k, q], cs.at[3 + 2 * k + q], cr.at[3 + 2 * (2 - k) + q], dev(y=ys[k]), sends)
        arrived(RZ0, cr.at[2])
        V0[...] = (T0[pl.ds(l * 4, 4)].astype(F32) + RZ0[...].astype(F32)).astype(BF16)
        for k in range(3):
            rcopy(V0.at[ys[k]], RY0.at[2 - k], cs.at[9 + k], cr.at[9 + 2 - k], dev(y=ys[k]), sends)
        for k in range(3):
            for q in range(2):
                arrived(RY1.at[k, q], cr.at[3 + 2 * k + q])
        total = [
            sum([RY1[k, q].astype(F32) for k in range(3)], T1[q * 4 + y].astype(F32)) for q in range(2)
        ]
        V1[...] = jnp.where(l == 0, total[1], total[0]).astype(BF16)
        rcopy(V1, RZ1, cs.at[12], cr.at[12], zp, sends)
        mine1 = jnp.where(l == 0, total[0], total[1])
        for k in range(3):
            arrived(RY0.at[k], cr.at[9 + k])
        RL0[layer] = sum([RY0[k].astype(F32) for k in range(3)], V0[y].astype(F32)).astype(BF16)
        arrived(RZ1, cr.at[12])
        RL1[layer] = (mine1 + RZ1[...].astype(F32)).astype(BF16)
        for cp in sends:
            cp.wait_send()

    def lcopy(p, m, ssem, to):
        r = (RL0, RL1)[p].at[m]
        return pltpu.make_async_remote_copy(r, r, ssem, lr.at[p, m], to, MESH)

    def lwait(p, m):
        arrived((RL0, RL1)[p].at[m], lr.at[p, m])

    ops = []

    @pl.when(x > 0)
    def _():
        lcopy(0, layer, ls.at[0], cross).start()
        for k in range(3):
            lcopy(1, layer, ls.at[1 + k], dev(x=xs[k])).start()
            lcopy(0, layer, ls.at[4 + k], dev(x=xs[k])).start()
        lcopy(1, layer, ls.at[7], cross).start()
        m = 2 * x + 1 - h
        lwait(0, m)
        for k in range(3):
            lcopy(0, m, ls.at[8 + k], dev(x=xs[k])).start()

    for k in (0, 2, 1):
        m = 2 * xs[k] + h

        @pl.when(xs[k] > 0)
        def _():
            lwait(1, m)
            lcopy(1, m, ls.at[11 + k], cross).start()

    for k in (0, 2, 1):

        @pl.when(xs[k] > 0)
        def _():
            lwait(0, 2 * xs[k] + h)
            lwait(0, 2 * xs[k] + 1 - h)
            lwait(1, 2 * xs[k] + 1 - h)

    @pl.when(x > 0)
    def _():
        lwait(1, 2 * x + 1 - h)

    for p, (RL, E) in enumerate(((RL0, E0), (RL1, E1))):
        for t in range(4):
            v = RL[place[PAIRS[t][0]]].astype(F32)
            for q in PAIRS[t][1:]:
                v = v + RL[place[q]].astype(F32)
            E[t] = v - tg[t, :, COL[p] : COL[p] + WIDE[p]]

    esends = []
    rcopy(E0.at[:, other, :], ER0, es.at[0], er.at[0], sib, esends)
    rcopy(E1.at[:, other, :], ER1, es.at[1], er.at[1], sib, esends)

    @pl.when(x > 0)
    def _():
        X0[c, u] = E0[mine_tgt].astype(BF16)
        X1[c, u] = E1[mine_tgt].astype(BF16)
        all_gather()

        def chunk(n, _):
            rows = pl.ds(pl.multiple_of(n * GC, GC), GC)
            v = against(rows).astype(BF16).reshape(8, ROWS, GC)
            GS[n] = v
            GR[layer, n] = GS[n, layer]
            for k in range(1, 8):
                m = lax.rem(layer + k, 8)
                pltpu.make_async_remote_copy(
                    GS.at[n, m], GR.at[layer, n], gs.at[n, k], gr.at[layer, n], (m, feat), MESH
                ).start()
            return 0

        lax.fori_loop(0, GN, chunk, 0)

    arrived(ER0, er.at[0])
    arrived(ER1, er.at[1])
    for p, (E, ER) in enumerate(((E0, ER0), (E1, ER1))):
        for cc in range(2):
            cols = slice(cc * HALF + COL[p], cc * HALF + COL[p] + WIDE[p])
            err_out[:, :, cols] = jnp.where(c == cc, E[:, own, :], ER[...])

    for m in range(2, 8):

        @pl.when(layer != m)
        def _():
            for n in range(GN):
                arrived(GR.at[m, n], gr.at[m, n])

    rows = pl.ds(pl.multiple_of(ROWS * layer, 8), ROWS)
    for s in range(2):
        for n in range(GN):
            v = GR[place[3 * s], n].astype(F32)
            for q in (1, 2):
                v = v + GR[place[3 * s + q], n].astype(F32)
            cols = slice(GC * n, GC * (n + 1))
            on = gate_of(jnp.concatenate([TK[s, rows, :]] * (GC // 128), axis=1), FC[s : s + 1, cols])
            pg_out[s, :, cols] = jnp.where(on, v, 0.0).astype(BF16)

    for cp in esends:
        cp.wait_send()

    @pl.when(x > 0)
    def _():
        lcopy(0, layer, ls.at[0], cross).wait_send()
        for k in range(3):
            lcopy(1, layer, ls.at[1 + k], dev(x=xs[k])).wait_send()
            lcopy(0, layer, ls.at[4 + k], dev(x=xs[k])).wait_send()
            lcopy(0, 2 * x + 1 - h, ls.at[8 + k], dev(x=xs[k])).wait_send()
        lcopy(1, layer, ls.at[7], cross).wait_send()

        def drain(n, _):
            for k in range(1, 8):
                m = lax.rem(layer + k, 8)
                pltpu.make_async_remote_copy(
                    GS.at[n, m], GR.at[layer, n], gs.at[n, k], gr.at[layer, n], (m, feat), MESH
                ).wait_send()
            return 0

        lax.fori_loop(0, GN, drain, 0)

    for k in range(3):

        @pl.when(xs[k] > 0)
        def _():
            lcopy(1, 2 * xs[k] + h, ls.at[11 + k], cross).wait_send()


def body(sources, targets, blocks, enc_bias, token_code, feature_threshold_code, dec_map):
    vm = pl.BlockSpec(memory_space=pltpu.VMEM)
    V = pltpu.VMEM
    D = pltpu.SemaphoreType.DMA
    w0, w1 = WIDE
    return pl.pallas_call(
        kernel,
        out_shape=(
            jax.ShapeDtypeStruct((4, 24, 4608), F32),
            jax.ShapeDtypeStruct((2, 48, 2048), BF16),
        ),
        in_specs=[pl.BlockSpec(memory_space=pltpu.SMEM), vm, vm, pl.BlockSpec(memory_space=pl.ANY), vm, vm, vm],
        out_specs=(vm, vm),
        scratch_shapes=[
            V((2048, 4608), BF16),
            V((2, 8, ROWS, w0), BF16),
            V((2, 8, ROWS, w1), BF16),
            V((2, NCH, 2, HR, CH), BF16),
            V((2, 384, HALF), F32),
            V((24, HALF), F32),
            V((ROWS, HALF), F32),
            V((4, 24, HALF), F32),
            V((4, ROWS, HALF), F32),
            V((2, 384, 128), F32),
            V((2, 2048), F32),
            V((8, ROWS, w0), BF16),
            V((8, ROWS, w1), BF16),
            V((8, ROWS, w0), BF16),
            V((8, ROWS, w1), BF16),
            V((8, ROWS, w0), BF16),
            V((8, ROWS, w1), BF16),
            V((4, ROWS, w0), BF16),
            V((3, 2, ROWS, w1), BF16),
            V((4, ROWS, w0), BF16),
            V((3, ROWS, w0), BF16),
            V((ROWS, w1), BF16),
            V((ROWS, w1), BF16),
            V((8, ROWS, w0), BF16),
            V((8, ROWS, w1), BF16),
            V((4, ROWS, w0), F32),
            V((4, ROWS, w1), F32),
            V((4, 24, w0), F32),
            V((4, 24, w1), F32),
            V((GN, 8, ROWS, GC), BF16),
            V((8, GN, ROWS, GC), BF16),
            D((NCH,)),
            D((4,)),
            D((32,)),
            D((2, 8)),
            D((2,)),
            D((2, 8)),
            D((2, NCH, 2)),
            D((NCH, 2)),
            D((2, NCH, 2)),
            D((13,)),
            D((13,)),
            D((14,)),
            D((2, 8)),
            D((2,)),
            D((2,)),
            D((GN, 8)),
            D((8, GN)),
        ],
        compiler_params=pltpu.CompilerParams(
            collective_id=1, has_side_effects=True, vmem_limit_bytes=61 * 2**20
        ),
        name="transcoder",
    )(dec_map, sources, targets, blocks, enc_bias, token_code, feature_threshold_code)


def solution(mesh):
    return jax.shard_map(
        body,
        mesh=mesh,
        in_specs=(
            P(None, "feat", None),
            P(None, "feat", None),
            P("layer", "feat", None),
            P(None, "feat"),
            P(),
            P(None, "feat"),
            P(),
        ),
        out_specs=(P(None, "feat", None), P(None, "layer", "feat")),
        check_vma=False,
    )
```

```python
import jax
import jax.numpy as jnp
from jax import lax
from jax.experimental import pallas as pl
from jax.experimental.pallas import tpu as pltpu
from jax.sharding import PartitionSpec as P

MESH = pl.DeviceIdType.MESH
F32 = jnp.float32
BF16 = jnp.bfloat16

ROWS = 48
HALF = 2304
GRP = 3
GW = 768
MID = 384
NCH = 8
CH = 256
SUB = 96
STEPS = 2 * NCH
CROSS0 = 3
FLAG = 5
LH = 3
ML = 12
GN = 8
GC = 256
GLAG = 3
ZG = 2

NT = (((1,), (1,)), ((), ()))
PAIRS = ((0,), (1, 3), (2, 4), (5,))


def gate_of(tok, code):
    v = tok * code
    q = jnp.floor(v * (1.0 / 251.0))
    return (v - 251.0 * q) < 40.0


def kernel(
    dm, src, tgt, w_hbm, bias, tok, fc, rec_out, pg_out,
    W, X, XO, FB, acc, sx_send, sx, tg_send, tg, TK, FC,
    S, C, T, RY, V1, RZ, R0, R1, R2, E, ER, GS, GA, GO, GC_, GZ,
    wsem, xsem, ags, agr, br, fs, fcs, fr, ss, sr, ys_s, ys_r, zs, zr, ls, lr, es, er, gs, gr, gzs, gzr,
):
    layer = lax.axis_index("layer")
    feat = lax.axis_index("feat")
    x, h = layer // 2, layer % 2
    l, y, c = feat // 8, (feat // 2) % 4, feat % 2
    o = 1 - c
    RL = (R0, R1, R2)

    def dev(x=x, h=h, l=l, y=y, c=c):
        return (2 * x + h, (4 * l + y) * 2 + c)

    ys = [lax.rem(y + k, 4) for k in (1, 2, 3)]
    xs = [lax.rem(x + k, 4) for k in (1, 2, 3)]
    sib = dev(c=o)
    zp = dev(l=1 - l)
    zo = dev(h=1 - h, l=1 - l)
    cross = dev(h=1 - h)

    def copy(a, b, ssem, rsem, to):
        return pltpu.make_async_remote_copy(
            src_ref=a, dst_ref=b, send_sem=ssem, recv_sem=rsem, device_id=to, device_id_type=MESH
        )

    def rcopy(a, b, ssem, rsem, to, sends):
        cp = copy(a, b, ssem, rsem, to)
        cp.start()
        sends.append(cp)

    def arrived(b, rsem):
        copy(b, b, rsem, rsem, sib).wait_recv()

    def half_of(v, which):
        return jnp.where(which == 0, v[..., :HALF], v[..., HALF:])

    own = pl.ds(pl.multiple_of(24 * c, 8), 24)
    other = pl.ds(pl.multiple_of(24 * o, 8), 24)

    def enter():
        bar = pltpu.get_barrier_semaphore()
        peers = [sib, zp, zo, cross] + [dev(y=a) for a in ys]
        peers += [dev(x=a) for a in xs] + [dev(x=a, h=1 - h) for a in xs]
        for p in peers:
            pl.semaphore_signal(bar, inc=1, device_id=p, device_id_type=MESH)
        for k in range(NCH):
            rows = pl.ds(CH * k, CH)
            pltpu.make_async_copy(w_hbm.at[0, rows], W.at[rows], wsem.at[k]).start()
        v = src[...].astype(F32)
        sx_send[...] = half_of(v, o)
        sx[:, own, :] = half_of(v, c)
        pl.semaphore_wait(bar, len(peers))

    def sources_in(sends):
        rcopy(sx_send, sx.at[:, own, :], xsem.at[0], xsem.at[1], sib, sends)
        arrived(sx.at[:, other, :], xsem.at[1])

    def targets_out(sends):
        for t in range(4):
            v = tgt[t].astype(F32)
            tg_send[t] = half_of(v, o)
            tg[t, own, :] = half_of(v, c)
        rcopy(tg_send, tg.at[:, own, :], xsem.at[2], xsem.at[3], sib, sends)

    def codes():
        for s in range(2):
            TK[s] = jnp.transpose(jnp.broadcast_to(tok[s : s + 1, :].astype(F32), (128, 384)))
        FC[...] = fc[...].astype(F32)

    yp, y2, ym = ys
    lo, hi = pl.ds(0, MID), pl.ds(MID, MID)
    count = [0]

    def gsend(src_ref, at, cols, to, rsem, sends):
        dst = X.at[at] if cols is None else X.at[at + (slice(None), cols)]
        a = src_ref if cols is None else src_ref.at[:, cols]
        rcopy(a, dst, ags.at[count[0]], rsem, to, sends)
        count[0] += 1

    def rsem_of(g, ll, yy, part=0):
        return agr.at[g, ll, yy, part]

    def both(g, ll, yy, sends):
        at = (c, g, ll, yy)
        gsend(X.at[at], at, None, sib, br.at[g, ll, yy], sends)

    def gather_first(g, sends):
        at = (c, g, l, y)
        r = X.at[at]
        for to in (yp, ym):
            gsend(r, at, None, dev(y=to), rsem_of(g, l, y), sends)
        if g == 0:
            gsend(XO.at[g], at, None, zo, rsem_of(g, l, y), sends)
        elif g == 1:
            gsend(r, at, None, zp, rsem_of(g, l, y), sends)
        else:
            gsend(XO.at[g], at, lo, zo, rsem_of(g, l, y, 0), sends)
            gsend(r, at, hi, zp, rsem_of(g, l, y, 1), sends)
        both(g, l, y, sends)

    def wait_z(g):
        if g < 2:
            arrived(X.at[c, g, 1 - l, y], rsem_of(g, 1 - l, y))
        else:
            arrived(X.at[c, g, 1 - l, y, :, lo], rsem_of(g, 1 - l, y, 0))
            arrived(X.at[c, g, 1 - l, y, :, hi], rsem_of(g, 1 - l, y, 1))

    def gather_own(sends):
        for g in range(GRP):
            for frm, to, cols, part in ((ym, yp, lo, 0), (yp, ym, hi, 1)):
                at = (c, g, l, frm)
                arrived(X.at[at], rsem_of(g, l, frm))
                gsend(X.at[at], at, cols, dev(y=to), rsem_of(g, l, frm, part), sends)
                both(g, l, frm, sends)
        for g in range(GRP):
            at = (c, g, 1 - l, y)
            wait_z(g)
            for to in (yp, ym, y2):
                gsend(X.at[at], at, None, dev(y=to), rsem_of(g, 1 - l, y), sends)
            both(g, 1 - l, y, sends)
        for g in range(GRP):
            arrived(X.at[c, g, l, y2, :, lo], rsem_of(g, l, y2, 0))
            arrived(X.at[c, g, l, y2, :, hi], rsem_of(g, l, y2, 1))
            both(g, l, y2, sends)
        for g in range(GRP):
            for yy in range(4):
                arrived(X.at[o, g, l, yy], br.at[g, l, yy])

    def gather_rest(sends):
        for g in range(GRP):
            for frm in (ym, yp, y2):
                arrived(X.at[c, g, 1 - l, frm], rsem_of(g, 1 - l, frm))
                both(g, 1 - l, frm, sends)
        for g in range(GRP):
            for yy in range(4):
                arrived(X.at[o, g, 1 - l, yy], br.at[g, 1 - l, yy])

    def errors_first(g, sends):
        at = (c, g, l, y)
        r = X.at[at]
        gsend(XO.at[g], at, None, zo, rsem_of(g, l, y), sends)
        for to in (yp, ym):
            gsend(r, at, None, dev(y=to), rsem_of(g, l, y), sends)
        both(g, l, y, sends)

    def from_y(g, ll, sends, on_z):
        for frm, to, cols, part in ((ym, yp, lo, 0), (yp, ym, hi, 1)):
            at = (c, g, ll, frm)
            arrived(X.at[at], rsem_of(g, ll, frm))
            gsend(X.at[at], at, cols, dev(y=to), rsem_of(g, ll, frm, part), sends)
            if on_z:
                gsend(X.at[at], at, None, zp, rsem_of(g, ll, frm), sends)
            both(g, ll, frm, sends)

    def from_y2(g, ll, sends, on_z):
        at = (c, g, ll, y2)
        arrived(X.at[at + (slice(None), lo)], rsem_of(g, ll, y2, 0))
        arrived(X.at[at + (slice(None), hi)], rsem_of(g, ll, y2, 1))
        if on_z:
            gsend(X.at[at], at, None, zp, rsem_of(g, ll, y2), sends)
        both(g, ll, y2, sends)

    def from_z(g, yy, sends, on_y):
        at = (c, g, 1 - l, yy)
        arrived(X.at[at], rsem_of(g, 1 - l, yy))
        if on_y:
            for to in (yp, ym):
                gsend(X.at[at], at, None, dev(y=to), rsem_of(g, 1 - l, yy), sends)
        both(g, 1 - l, yy, sends)

    def gather_errors(sends):
        from_z(0, y, sends, True)
        from_y(0, l, sends, False)
        from_y(1, l, sends, True)
        from_y(2, l, sends, True)
        from_y(0, 1 - l, sends, False)
        from_y2(1, l, sends, True)
        from_y2(2, l, sends, True)
        from_y2(0, l, sends, False)
        from_z(1, y, sends, False)
        from_z(2, y, sends, False)
        for g in (1, 2):
            for yy in (ym, yp):
                from_z(g, yy, sends, False)
        from_y2(0, 1 - l, sends, False)
        for g in (1, 2):
            from_z(g, y2, sends, False)
        for g in range(GRP):
            for ll in range(2):
                for yy in range(4):
                    arrived(X.at[o, g, ll, yy], br.at[g, ll, yy])

    def against(lh, rows):
        total = None
        for cc in range(2):
            for g in range(GRP):
                a = X[cc, g].reshape(384, GW) if lh is None else X[cc, g, lh].reshape(192, GW)
                b = W[rows, cc * HALF + g * GW : cc * HALF + (g + 1) * GW]
                d = lax.dot_general(a, b, NT, preferred_element_type=F32)
                total = d if total is None else total + d
        return total

    def piece(s, i):
        return s, lax.rem(l + i // NCH, 2), lax.rem(i, NCH)

    def fcopy(s, i, way, to, sem=None):
        s, lh, k = piece(s, i)
        r = FB.at[s, lh, k, way]
        return copy(r, r, (fs if sem is None else sem).at[s, lh, k, way], fr.at[s, lh, k, way], to)

    def farrived(s, i, way):
        s, lh, k = piece(s, i)
        arrived(FB.at[s, lh, k, way], fr.at[s, lh, k, way])

    def crosses0(i):
        return lax.rem(i, NCH) < CROSS0

    def encode():
        sends = []
        sources_in(sends)
        for g in range(GRP):
            cols = slice(GW * g, GW * (g + 1))
            X[c, g, l, y] = sx[h, :, cols].astype(BF16)
            XO[g] = sx[1 - h, :, cols].astype(BF16)
            gather_first(g, sends)
        targets_out(sends)
        codes()
        gather_own(sends)
        line = (dev(x=1), dev(x=3))

        def chunk(i, _):
            _, lh, k = piece(h, i)
            rows = pl.ds(pl.multiple_of(k * CH, CH), CH)

            @pl.when(i < NCH)
            def _():
                pltpu.make_async_copy(w_hbm.at[0, rows], W.at[rows], wsem.at[k]).wait()

            pre = against(lh, rows) + bias[pl.ds(h, 1), rows]
            toks = TK[h, pl.ds(pl.multiple_of(lh * 192, 8), 192), :]
            on = gate_of(jnp.concatenate([toks] * 2, axis=1), FC[pl.ds(h, 1), rows])
            FB[h, lh, k] = jnp.where(on, pre, 0.0).astype(BF16).reshape(2, SUB, CH)
            for way in range(2):
                fcopy(h, i, way, line[way]).start()

            @pl.when(crosses0(i))
            def _():
                for way in range(2):
                    fcopy(h, i, way, cross, fcs).start()

            j = i - FLAG

            @pl.when((j >= 0) & crosses0(j + NCH))
            def _():
                for way in range(2):
                    farrived(1 - h, j, way)
                    fcopy(1 - h, j, way, line[way]).start()

            return 0

        lax.fori_loop(0, NCH, chunk, 0)
        gather_rest(sends)
        lax.fori_loop(NCH, STEPS, chunk, 0)

        def drain(i, _):
            for way in range(2):
                fcopy(h, i, way, line[way]).wait_send()

                @pl.when(crosses0(i))
                def _():
                    fcopy(h, i, way, cross, fcs).wait_send()
                    fcopy(1 - h, i, way, line[way]).wait_send()

            return 0

        lax.fori_loop(0, STEPS, drain, 0)
        for cp in sends:
            cp.wait_send()
        arrived(tg.at[:, other, :], xsem.at[3])

    def lh_of(j):
        return l if j == 0 else 1 - l

    def fold_start(j, sends):
        for g in range(GRP):
            cols = slice(GW * g, GW * (g + 1))
            S[j, g] = acc[o, lh_of(j), :, cols].astype(BF16).reshape(4, ROWS, GW)
            rcopy(S.at[j, g], C.at[j, g], ss.at[j, g], sr.at[j, g], sib, sends)

    def fold_end(j, sends):
        for g in range(GRP):
            cols = slice(GW * g, GW * (g + 1))
            arrived(C.at[j, g], sr.at[j, g])
            v = acc[c, lh_of(j), :, cols] + C[j, g].astype(F32).reshape(192, GW)
            T[j, g] = v.astype(BF16).reshape(4, ROWS, GW)
            for k in (0, 2, 1):
                rcopy(T.at[j, g, ys[k]], RY.at[j, g, 2 - k], ys_s.at[j, g, k], ys_r.at[j, g, 2 - k], dev(y=ys[k]), sends)

    def fold_sum(j, g):
        for k in range(3):
            arrived(RY.at[j, g, k], ys_r.at[j, g, k])
        v = T[j, g, y].astype(F32)
        for k in range(3):
            v = v + RY[j, g, k].astype(F32)
        return v

    def decode():
        sends = []
        acc[...] = jnp.zeros_like(acc)
        xin = []
        sources_in(xin)
        targets_out(xin)
        codes()
        nxt = (dev(x=lax.rem(x + 1, 4)), dev(x=lax.rem(x + 3, 4)))
        more = (x < 3, x > 1)
        lag = ((x - 1) * LH, (3 - x) * LH)
        mine_src = (dm[layer - 2] >= 3).astype(jnp.int32)

        def step(t, _):
            for way in range(2):
                i = t - lag[way]

                @pl.when((i >= 0) & (i < STEPS))
                def _():
                    farrived(h, i, way)

                    @pl.when(more[way])
                    def _():
                        fcopy(h, i, way, nxt[way]).start()

                    @pl.when(jnp.logical_not(crosses0(i)))
                    def _():
                        fcopy(h, i, way, cross, fcs).start()

                j = i - FLAG

                @pl.when((j >= 0) & (j < STEPS) & crosses0(j + 2 * NCH))
                def _():
                    farrived(1 - h, j, way)

                    @pl.when(more[way])
                    def _():
                        fcopy(1 - h, j, way, nxt[way]).start()

            m = t - ML

            @pl.when(m >= 0)
            def _():
                @pl.when(jnp.logical_not(crosses0(m)))
                def _():
                    for way in range(2):
                        farrived(1 - h, m, way)

                _, lh, k = piece(h, m)
                rows = pl.ds(pl.multiple_of(k * CH, CH), CH)

                @pl.when(m < NCH)
                def _():
                    pltpu.make_async_copy(w_hbm.at[0, rows], W.at[rows], wsem.at[k]).wait()

                a = jnp.where(mine_src == 0, FB[0, lh, k], FB[1, lh, k]).reshape(192, CH)
                for cc in range(2):
                    for n in range(GRP):
                        cols = slice(cc * HALF + n * GW, cc * HALF + (n + 1) * GW)
                        acc[cc, lh, :, n * GW : (n + 1) * GW] += jnp.dot(a, W[rows, cols], preferred_element_type=F32)

            return 0

        lax.fori_loop(0, NCH + ML, step, 0)
        fold_start(0, sends)
        lax.fori_loop(NCH + ML, NCH + ML + 2, step, 0)
        fold_end(0, sends)
        lax.fori_loop(NCH + ML + 2, STEPS + ML, step, 0)
        fold_start(1, sends)
        fold_end(1, sends)

        def drain(i, _):
            for way in range(2):

                @pl.when(more[way])
                def _():
                    fcopy(h, i, way, nxt[way]).wait_send()

                    @pl.when(crosses0(i))
                    def _():
                        fcopy(1 - h, i, way, nxt[way]).wait_send()

                @pl.when(jnp.logical_not(crosses0(i)))
                def _():
                    fcopy(h, i, way, cross, fcs).wait_send()

            return 0

        lax.fori_loop(0, STEPS, drain, 0)
        for cp in xin:
            cp.wait_send()
        arrived(tg.at[:, other, :], xsem.at[3])
        for g in range(GRP + 1):
            if g < GRP:
                V1[g] = fold_sum(1, g).astype(BF16)
                rcopy(V1.at[g], RZ.at[g], zs.at[g], zr.at[g], zp, sends)
            if g > 0:
                v = fold_sum(0, g - 1)
                arrived(RZ.at[g - 1], zr.at[g - 1])
                RL[g - 1][layer] = (v + RZ[g - 1].astype(F32)).astype(BF16)
                lcopy(g - 1, layer, 0, cross).start()
                for k in range(3):
                    lcopy(g - 1, layer, 1 + k, dev(x=xs[k])).start()
        for cp in sends:
            cp.wait_send()

    def lcopy(g, m, n, to):
        r = RL[g].at[m]
        return copy(r, r, ls.at[g, n], lr.at[g, m], to)

    def lwait(g, m):
        arrived(RL[g].at[m], lr.at[g, m])

    def exchange(g):
        pair = 2 * x + 1 - h
        if g == ZG:

            @pl.when(x > 0)
            def _():
                lwait(g, pair)
                for k in range(3):
                    lcopy(g, pair, 4 + k, dev(x=xs[k])).start()

        else:
            for k in (0, 2, 1):

                @pl.when(xs[k] > 0)
                def _():
                    m = 2 * xs[k] + h
                    lwait(g, m)
                    lcopy(g, m, 4 + k, cross).start()

    def exchanged(g):
        for k in range(3):

            @pl.when(xs[k] > 0)
            def _():
                lwait(g, 2 * xs[k] + 1 - h)
                if g == ZG:
                    lwait(g, 2 * xs[k] + h)

        if g != ZG:

            @pl.when(x > 0)
            def _():
                lwait(g, 2 * x + 1 - h)

    def exchange_drain():
        @pl.when(x > 0)
        def _():
            for g in range(GRP):
                lcopy(g, layer, 0, cross).wait_send()
                for k in range(3):
                    lcopy(g, layer, 1 + k, dev(x=xs[k])).wait_send()
            for k in range(3):
                lcopy(ZG, 2 * x + 1 - h, 4 + k, dev(x=xs[k])).wait_send()

        for g in range(GRP):
            if g == ZG:
                continue
            for k in range(3):

                @pl.when(xs[k] > 0)
                def _():
                    lcopy(g, 2 * xs[k] + h, 4 + k, cross).wait_send()

    place = []
    for p in range(6):
        at = jnp.int32(2)
        for i in range(6):
            at = jnp.where(dm[i] == p, jnp.int32(i + 2), at)
        place.append(at)

    def target_of(m):
        pair = dm[jnp.maximum(m - 2, 0)]
        return jnp.where(pair >= 3, pair - 2, pair)

    def recon(g, sends):
        for t in range(4):
            v = RL[g][place[PAIRS[t][0]]].astype(F32)
            for q in PAIRS[t][1:]:
                v = v + RL[g][place[q]].astype(F32)
            E[g, t] = v
        rcopy(E.at[g, :, other, :], ER.at[g], es.at[g], er.at[g], sib, sends)

    def recon_out():
        for g in range(GRP):
            arrived(ER.at[g], er.at[g])
            for cc in range(2):
                cols = slice(cc * HALF + GW * g, cc * HALF + GW * (g + 1))
                rec_out[:, :, cols] = jnp.where(c == cc, E[g, :, own, :], ER[g])

    def gcopy(n, k):
        to = xs[k]
        return copy(GS.at[n, pl.ds(2 * to, 2)], GA.at[n, x], gs.at[n, k], gr.at[n, x], dev(x=to))

    def zcopy(n):
        return copy(GC_.at[n], GZ.at[n], gzs.at[n], gzr.at[n], cross)

    def line_sum(n):
        for k in range(3):

            @pl.when(xs[k] > 0)
            def _():
                arrived(GA.at[n, xs[k]], gr.at[n, xs[k]])

        for s in range(2):
            mine, far = None, None
            for a in range(1, 4):
                on = (dm[2 * a + h - 2] >= 3) == (s == 1)
                p = jnp.where(on, GA[n, a, h].astype(F32), 0.0)
                q = jnp.where(on, GA[n, a, 1 - h].astype(F32), 0.0)
                mine = p if mine is None else mine + p
                far = q if far is None else far + q
            GO[n, s] = mine
            GC_[n, s] = far.astype(BF16)
        zcopy(n).start()

    def grads():
        def chunk(n, _):
            rows = pl.ds(pl.multiple_of(n * GC, GC), GC)
            GS[n] = against(None, rows).astype(BF16).reshape(8, ROWS, GC)
            for k in (0, 2, 1):
                gcopy(n, k).start()
            GA[n, x] = GS[n, pl.ds(2 * x, 2)]

            @pl.when(n >= GLAG)
            def _():
                line_sum(n - GLAG)

            return 0

        lax.fori_loop(0, GN, chunk, 0)

    def line_sums(start):
        def one(n, _):
            line_sum(n)
            return 0

        lax.fori_loop(start, GN, one, 0)

    def grads_drain():
        def drain(n, _):
            for k in range(3):
                gcopy(n, k).wait_send()
            return 0

        lax.fori_loop(0, GN, drain, 0)

    def grads_out():
        rows = pl.ds(pl.multiple_of(ROWS * layer, 8), ROWS)
        for n in range(GN):
            cols = slice(GC * n, GC * (n + 1))
            arrived(GZ.at[n], gzr.at[n])
            for s in range(2):
                v = GO[n, s] + GZ[n, s].astype(F32)
                on = gate_of(jnp.concatenate([TK[s, rows, :]] * (GC // 128), axis=1), FC[s : s + 1, cols])
                pg_out[s, :, cols] = jnp.where(on, v, 0.0).astype(BF16)
        for n in range(GN):
            zcopy(n).wait_send()

    def error_block(g, sends):
        cols = slice(GW * g, GW * (g + 1))
        for dst, t in ((X.at[c, g, l, y], target_of(layer)), (XO.at[g], target_of(2 * x + 1 - h))):
            dst[...] = (E[g, t] - tg[t, :, cols]).astype(BF16)
        errors_first(g, sends)

    def decoder_rest():
        sends = []
        count[0] = 0
        for g in range(GRP):
            exchange(g)
        for g in range(GRP):
            exchanged(g)
            recon(g, sends)
            error_block(g, sends)
        gather_errors(sends)
        grads()
        recon_out()
        line_sums(GN - GLAG)
        for cp in sends:
            cp.wait_send()
        grads_drain()

    def encoder_rest():
        sends = []
        for g in range(GRP):
            exchange(g)
        for g in range(GRP):
            exchanged(g)
            recon(g, sends)
        recon_out()
        line_sums(0)
        for cp in sends:
            cp.wait_send()

    enter()
    pl.when(x == 0)(encode)
    pl.when(x > 0)(decode)
    pl.when(x > 0)(decoder_rest)
    pl.when(x == 0)(encoder_rest)
    grads_out()
    exchange_drain()


def body(sources, targets, blocks, enc_bias, token_code, feature_threshold_code, dec_map):
    vm = pl.BlockSpec(memory_space=pltpu.VMEM)
    V = pltpu.VMEM
    D = pltpu.SemaphoreType.DMA
    recon, pre_grads = pl.pallas_call(
        kernel,
        out_shape=(
            jax.ShapeDtypeStruct((4, 24, 4608), F32),
            jax.ShapeDtypeStruct((2, 48, 2048), BF16),
        ),
        in_specs=[pl.BlockSpec(memory_space=pltpu.SMEM), vm, vm, pl.BlockSpec(memory_space=pl.ANY), vm, vm, vm],
        out_specs=(vm, vm),
        scratch_shapes=[
            V((2048, 4608), BF16),
            V((2, GRP, 2, 4, ROWS, GW), BF16),
            V((GRP, ROWS, GW), BF16),
            V((2, 2, NCH, 2, SUB, CH), BF16),
            V((2, 2, 192, HALF), F32),
            V((2, 24, HALF), F32),
            V((2, ROWS, HALF), F32),
            V((4, 24, HALF), F32),
            V((4, ROWS, HALF), F32),
            V((2, 384, 128), F32),
            V((2, 2048), F32),
            V((2, GRP, 4, ROWS, GW), BF16),
            V((2, GRP, 4, ROWS, GW), BF16),
            V((2, GRP, 4, ROWS, GW), BF16),
            V((2, GRP, 3, ROWS, GW), BF16),
            V((GRP, ROWS, GW), BF16),
            V((GRP, ROWS, GW), BF16),
            V((8, ROWS, GW), BF16),
            V((8, ROWS, GW), BF16),
            V((8, ROWS, GW), BF16),
            V((GRP, 4, ROWS, GW), F32),
            V((GRP, 4, 24, GW), F32),
            V((GN, 8, ROWS, GC), BF16),
            V((GN, 4, 2, ROWS, GC), BF16),
            V((GN, 2, ROWS, GC), F32),
            V((GN, 2, ROWS, GC), BF16),
            V((GN, 2, ROWS, GC), BF16),
            D((NCH,)),
            D((4,)),
            D((64,)),
            D((GRP, 2, 4, 2)),
            D((GRP, 2, 4)),
            D((2, 2, NCH, 2)),
            D((2, 2, NCH, 2)),
            D((2, 2, NCH, 2)),
            D((2, GRP)),
            D((2, GRP)),
            D((2, GRP, 3)),
            D((2, GRP, 3)),
            D((GRP,)),
            D((GRP,)),
            D((GRP, 7)),
            D((GRP, 8)),
            D((GRP,)),
            D((GRP,)),
            D((GN, 3)),
            D((GN, 4)),
            D((GN,)),
            D((GN,)),
        ],
        compiler_params=pltpu.CompilerParams(
            collective_id=1, has_side_effects=True, vmem_limit_bytes=62 * 2**20
        ),
        name="transcoder",
    )(dec_map, sources, targets, blocks, enc_bias, token_code, feature_threshold_code)
    return recon - targets.astype(F32), pre_grads


def solution(mesh):
    return jax.shard_map(
        body,
        mesh=mesh,
        in_specs=(
            P(None, "feat", None),
            P(None, "feat", None),
            P("layer", "feat", None),
            P(None, "feat"),
            P(),
            P(None, "feat"),
            P(),
        ),
        out_specs=(P(None, "feat", None), P(None, "layer", "feat")),
        check_vma=False,
    )
```

```python
import jax
import jax.numpy as jnp
from jax import lax
from jax.experimental import pallas as pl
from jax.experimental.pallas import tpu as pltpu
from jax.sharding import PartitionSpec as P

MESH = pl.DeviceIdType.MESH
F32 = jnp.float32
BF16 = jnp.bfloat16

ROWS = 48
HALF = 2304
GRP = 6
GW = 384
DW = 768
NCH = 8
CH = 256
SUB = 96
STEPS = 2 * NCH
CROSS0 = 3
FLAG = 5
LH = 3
ML = 12
GN = 8
GC = 256
GLAG = 3
ZG = (3, 4, 5)
LC = 2
LX = 5
LE = 9
GL = 3

NT = (((1,), (1,)), ((), ()))
PAIRS = ((0,), (1, 3), (2, 4), (5,))


def gate_of(tok, code):
    v = tok * code
    q = jnp.floor(v * (1.0 / 251.0))
    return (v - 251.0 * q) < 40.0


def kernel(
    dm, src, tgt, w_hbm, bias, tok, fc, rec_out, pg_out,
    W, X, XO, FB, acc, sx_send, sx, tg_send, tg, TK, FC,
    S, C, T, RY, V1, RZ, R0, R1, R2, R3, R4, R5, E, ER, RO, GS, GA, GO, GC_, GZ,
    wsem, xsem, ags, agr, br, fs, fcs, fr, ss, sr, ys_s, ys_r, zs, zr, ls, lr, es, er, gs, gr, gzs, gzr, osem,
):
    layer = lax.axis_index("layer")
    feat = lax.axis_index("feat")
    x, h = layer // 2, layer % 2
    l, y, c = feat // 8, (feat // 2) % 4, feat % 2
    o = 1 - c
    RL = (R0, R1, R2, R3, R4, R5)

    def dev(x=x, h=h, l=l, y=y, c=c):
        return (2 * x + h, (4 * l + y) * 2 + c)

    ys = [lax.rem(y + k, 4) for k in (1, 2, 3)]
    xs = [lax.rem(x + k, 4) for k in (1, 2, 3)]
    sib = dev(c=o)
    zp = dev(l=1 - l)
    zo = dev(h=1 - h, l=1 - l)
    cross = dev(h=1 - h)

    def copy(a, b, ssem, rsem, to):
        return pltpu.make_async_remote_copy(
            src_ref=a, dst_ref=b, send_sem=ssem, recv_sem=rsem, device_id=to, device_id_type=MESH
        )

    def rcopy(a, b, ssem, rsem, to, sends):
        cp = copy(a, b, ssem, rsem, to)
        cp.start()
        sends.append(cp)

    def arrived(b, rsem):
        copy(b, b, rsem, rsem, sib).wait_recv()

    def half_of(v, which):
        return jnp.where(which == 0, v[..., :HALF], v[..., HALF:])

    own = pl.ds(pl.multiple_of(24 * c, 8), 24)
    other = pl.ds(pl.multiple_of(24 * o, 8), 24)

    def enter():
        bar = pltpu.get_barrier_semaphore()
        peers = [sib, zp, zo, cross] + [dev(y=a) for a in ys]
        peers += [dev(x=a) for a in xs] + [dev(x=a, h=1 - h) for a in xs]
        for p in peers:
            pl.semaphore_signal(bar, inc=1, device_id=p, device_id_type=MESH)
        for k in range(NCH):
            rows = pl.ds(CH * k, CH)
            pltpu.make_async_copy(w_hbm.at[0, rows], W.at[rows], wsem.at[k]).start()
        v = src[...].astype(F32)
        sx_send[...] = half_of(v, o)
        sx[:, own, :] = half_of(v, c)
        pl.semaphore_wait(bar, len(peers))

    def sources_in(sends):
        rcopy(sx_send, sx.at[:, own, :], xsem.at[0], xsem.at[1], sib, sends)
        arrived(sx.at[:, other, :], xsem.at[1])

    def targets_out(sends):
        for t in range(4):
            v = tgt[t].astype(F32)
            tg_send[t] = half_of(v, o)
            tg[t, own, :] = half_of(v, c)
        rcopy(tg_send, tg.at[:, own, :], xsem.at[2], xsem.at[3], sib, sends)

    def codes():
        for s in range(2):
            TK[s] = jnp.transpose(jnp.broadcast_to(tok[s : s + 1, :].astype(F32), (128, 384)))
        FC[...] = fc[...].astype(F32)

    yp, y2, ym = ys

    def parts(g):
        m = 128 if g % 2 == 0 else 256
        return pl.ds(0, m), pl.ds(m, GW - m)

    count = [0]

    def gsend(src_ref, at, cols, to, rsem, sends):
        dst = X.at[at] if cols is None else X.at[at + (slice(None), cols)]
        a = src_ref if cols is None else src_ref.at[:, cols]
        rcopy(a, dst, ags.at[count[0]], rsem, to, sends)
        count[0] += 1

    def rsem_of(g, ll, yy, part=0):
        return agr.at[g, ll, yy, part]

    def both(g, ll, yy, sends):
        at = (c, g, ll, yy)
        gsend(X.at[at], at, None, sib, br.at[g, ll, yy], sends)

    def gather_first(g, sends):
        at = (c, g, l, y)
        r = X.at[at]
        for to in (yp, ym):
            gsend(r, at, None, dev(y=to), rsem_of(g, l, y), sends)
        if g % 2 == 0:
            gsend(XO.at[g], at, None, zo, rsem_of(g, l, y), sends)
        else:
            gsend(r, at, None, zp, rsem_of(g, l, y), sends)
        both(g, l, y, sends)

    def gather_own(sends):
        for g in range(GRP):
            lo, hi = parts(g)
            for frm, to, cols, part in ((ym, yp, lo, 0), (yp, ym, hi, 1)):
                at = (c, g, l, frm)
                arrived(X.at[at], rsem_of(g, l, frm))
                gsend(X.at[at], at, cols, dev(y=to), rsem_of(g, l, frm, part), sends)
                both(g, l, frm, sends)
        for g in range(GRP):
            at = (c, g, 1 - l, y)
            arrived(X.at[at], rsem_of(g, 1 - l, y))
            for to in (yp, ym, y2):
                gsend(X.at[at], at, None, dev(y=to), rsem_of(g, 1 - l, y), sends)
            both(g, 1 - l, y, sends)
        for g in range(GRP):
            lo, hi = parts(g)
            arrived(X.at[c, g, l, y2, :, lo], rsem_of(g, l, y2, 0))
            arrived(X.at[c, g, l, y2, :, hi], rsem_of(g, l, y2, 1))
            both(g, l, y2, sends)
        for g in range(GRP):
            for yy in range(4):
                arrived(X.at[o, g, l, yy], br.at[g, l, yy])

    def gather_rest(sends):
        for g in range(GRP):
            for frm in (ym, yp, y2):
                arrived(X.at[c, g, 1 - l, frm], rsem_of(g, 1 - l, frm))
                both(g, 1 - l, frm, sends)
        for g in range(GRP):
            for yy in range(4):
                arrived(X.at[o, g, 1 - l, yy], br.at[g, 1 - l, yy])

    def errors_first(g, sends):
        at = (c, g, l, y)
        r = X.at[at]
        gsend(XO.at[g], at, None, zo, rsem_of(g, l, y), sends)
        for to in (yp, ym):
            gsend(r, at, None, dev(y=to), rsem_of(g, l, y), sends)
        both(g, l, y, sends)

    def from_y(g, ll, sends, on_z):
        lo, hi = parts(g)
        for frm, to, cols, part in ((ym, yp, lo, 0), (yp, ym, hi, 1)):
            at = (c, g, ll, frm)
            arrived(X.at[at], rsem_of(g, ll, frm))
            gsend(X.at[at], at, cols, dev(y=to), rsem_of(g, ll, frm, part), sends)
            if on_z:
                gsend(X.at[at], at, None, zp, rsem_of(g, ll, frm), sends)
            both(g, ll, frm, sends)

    def from_y2(g, ll, sends, on_z):
        lo, hi = parts(g)
        at = (c, g, ll, y2)
        arrived(X.at[at + (slice(None), lo)], rsem_of(g, ll, y2, 0))
        arrived(X.at[at + (slice(None), hi)], rsem_of(g, ll, y2, 1))
        if on_z:
            gsend(X.at[at], at, None, zp, rsem_of(g, ll, y2), sends)
        both(g, ll, y2, sends)

    def from_z(g, yy, sends, on_y):
        at = (c, g, 1 - l, yy)
        arrived(X.at[at], rsem_of(g, 1 - l, yy))
        if on_y:
            for to in (yp, ym):
                gsend(X.at[at], at, None, dev(y=to), rsem_of(g, 1 - l, yy), sends)
        both(g, 1 - l, yy, sends)

    def gather_errors(g, n, sends):
        if g in ZG:
            if n == 0:
                from_z(g, y, sends, True)
                from_y(g, l, sends, False)
            elif n == 1:
                from_y(g, 1 - l, sends, False)
                from_y2(g, l, sends, False)
            elif n == 2:
                from_y2(g, 1 - l, sends, False)
        elif n == 0:
            from_y(g, l, sends, True)
        elif n == 1:
            from_y2(g, l, sends, True)
            from_z(g, y, sends, False)
        elif n == 2:
            from_z(g, ym, sends, False)
            from_z(g, yp, sends, False)
        else:
            from_z(g, y2, sends, False)

    def gathered():
        for g in range(GRP):
            for ll in range(2):
                for yy in range(4):
                    arrived(X.at[o, g, ll, yy], br.at[g, ll, yy])

    def against(lh, rows):
        total = None
        for cc in range(2):
            for n in range(HALF // DW):
                a = [X[cc, g] if lh is None else X[cc, g, lh] for g in (2 * n, 2 * n + 1)]
                a = jnp.concatenate([v.reshape(-1, GW) for v in a], axis=1)
                b = W[rows, cc * HALF + n * DW : cc * HALF + (n + 1) * DW]
                d = lax.dot_general(a, b, NT, preferred_element_type=F32)
                total = d if total is None else total + d
        return total

    def piece(s, i):
        return s, lax.rem(l + i // NCH, 2), lax.rem(i, NCH)

    def fcopy(s, i, way, to, sem=None):
        s, lh, k = piece(s, i)
        r = FB.at[s, lh, k, way]
        return copy(r, r, (fs if sem is None else sem).at[s, lh, k, way], fr.at[s, lh, k, way], to)

    def farrived(s, i, way):
        s, lh, k = piece(s, i)
        arrived(FB.at[s, lh, k, way], fr.at[s, lh, k, way])

    def crosses0(i):
        return lax.rem(i, NCH) < CROSS0

    def encode():
        sends = []
        sources_in(sends)
        for g in range(GRP):
            cols = slice(GW * g, GW * (g + 1))
            X[c, g, l, y] = sx[h, :, cols].astype(BF16)
            XO[g] = sx[1 - h, :, cols].astype(BF16)
            gather_first(g, sends)
        targets_out(sends)
        codes()
        gather_own(sends)
        line = (dev(x=1), dev(x=3))

        def chunk(i, _):
            _, lh, k = piece(h, i)
            rows = pl.ds(pl.multiple_of(k * CH, CH), CH)

            @pl.when(i < NCH)
            def _():
                pltpu.make_async_copy(w_hbm.at[0, rows], W.at[rows], wsem.at[k]).wait()

            pre = against(lh, rows) + bias[pl.ds(h, 1), rows]
            toks = TK[h, pl.ds(pl.multiple_of(lh * 192, 8), 192), :]
            on = gate_of(jnp.concatenate([toks] * 2, axis=1), FC[pl.ds(h, 1), rows])
            FB[h, lh, k] = jnp.where(on, pre, 0.0).astype(BF16).reshape(2, SUB, CH)
            for way in range(2):
                fcopy(h, i, way, line[way]).start()

            @pl.when(crosses0(i))
            def _():
                for way in range(2):
                    fcopy(h, i, way, cross, fcs).start()

            j = i - FLAG

            @pl.when((j >= 0) & crosses0(j + NCH))
            def _():
                for way in range(2):
                    farrived(1 - h, j, way)
                    fcopy(1 - h, j, way, line[way]).start()

            return 0

        lax.fori_loop(0, NCH, chunk, 0)
        gather_rest(sends)
        lax.fori_loop(NCH, STEPS, chunk, 0)

        def drain(i, _):
            for way in range(2):
                fcopy(h, i, way, line[way]).wait_send()

                @pl.when(crosses0(i))
                def _():
                    fcopy(h, i, way, cross, fcs).wait_send()
                    fcopy(1 - h, i, way, line[way]).wait_send()

            return 0

        lax.fori_loop(0, STEPS, drain, 0)
        for cp in sends:
            cp.wait_send()
        arrived(tg.at[:, other, :], xsem.at[3])

    def lh_of(j):
        return l if j == 0 else 1 - l

    def fold_start(j, sends):
        for g in range(GRP):
            cols = slice(GW * g, GW * (g + 1))
            S[j, g] = acc[o, lh_of(j), :, cols].astype(BF16).reshape(4, ROWS, GW)
            rcopy(S.at[j, g], C.at[j, g], ss.at[j, g], sr.at[j, g], sib, sends)

    def fold_end(j, sends):
        for g in range(GRP):
            cols = slice(GW * g, GW * (g + 1))
            arrived(C.at[j, g], sr.at[j, g])
            v = acc[c, lh_of(j), :, cols] + C[j, g].astype(F32).reshape(192, GW)
            T[j, g] = v.astype(BF16).reshape(4, ROWS, GW)
            for k in (0, 2, 1):
                rcopy(T.at[j, g, ys[k]], RY.at[j, g, 2 - k], ys_s.at[j, g, k], ys_r.at[j, g, 2 - k], dev(y=ys[k]), sends)

    def fold_sum(j, g):
        for k in range(3):
            arrived(RY.at[j, g, k], ys_r.at[j, g, k])
        v = T[j, g, y].astype(F32)
        for k in range(3):
            v = v + RY[j, g, k].astype(F32)
        return v

    def decode():
        sends = []
        acc[...] = jnp.zeros_like(acc)
        xin = []
        sources_in(xin)
        targets_out(xin)
        codes()
        nxt = (dev(x=lax.rem(x + 1, 4)), dev(x=lax.rem(x + 3, 4)))
        more = (x < 3, x > 1)
        lag = ((x - 1) * LH, (3 - x) * LH)
        mine_src = (dm[layer - 2] >= 3).astype(jnp.int32)

        def step(t, _):
            for way in range(2):
                i = t - lag[way]

                @pl.when((i >= 0) & (i < STEPS))
                def _():
                    farrived(h, i, way)

                    @pl.when(more[way])
                    def _():
                        fcopy(h, i, way, nxt[way]).start()

                    @pl.when(jnp.logical_not(crosses0(i)))
                    def _():
                        fcopy(h, i, way, cross, fcs).start()

                j = i - FLAG

                @pl.when((j >= 0) & (j < STEPS) & crosses0(j + 2 * NCH))
                def _():
                    farrived(1 - h, j, way)

                    @pl.when(more[way])
                    def _():
                        fcopy(1 - h, j, way, nxt[way]).start()

            m = t - ML

            @pl.when(m >= 0)
            def _():
                @pl.when(jnp.logical_not(crosses0(m)))
                def _():
                    for way in range(2):
                        farrived(1 - h, m, way)

                _, lh, k = piece(h, m)
                rows = pl.ds(pl.multiple_of(k * CH, CH), CH)

                @pl.when(m < NCH)
                def _():
                    pltpu.make_async_copy(w_hbm.at[0, rows], W.at[rows], wsem.at[k]).wait()

                a = jnp.where(mine_src == 0, FB[0, lh, k], FB[1, lh, k]).reshape(192, CH)
                for cc in range(2):
                    for n in range(HALF // DW):
                        cols = slice(cc * HALF + n * DW, cc * HALF + (n + 1) * DW)
                        acc[cc, lh, :, n * DW : (n + 1) * DW] += jnp.dot(a, W[rows, cols], preferred_element_type=F32)

            return 0

        lax.fori_loop(0, NCH + ML, step, 0)
        fold_start(0, sends)
        lax.fori_loop(NCH + ML, NCH + ML + 2, step, 0)
        fold_end(0, sends)
        lax.fori_loop(NCH + ML + 2, STEPS + ML, step, 0)
        fold_start(1, sends)
        fold_end(1, sends)

        arrived(tg.at[:, other, :], xsem.at[3])
        count[0] = 0
        for t in range(GRP + LE + 4 * GL):
            g = t
            if g < GRP:
                V1[g] = fold_sum(1, g).astype(BF16)
                rcopy(V1.at[g], RZ.at[g], zs.at[g], zr.at[g], zp, sends)
            g = t - LC
            if 0 <= g < GRP:
                v = fold_sum(0, g)
                arrived(RZ.at[g], zr.at[g])
                RL[g][layer] = (v + RZ[g].astype(F32)).astype(BF16)
                lcopy(g, layer, 0, cross).start()
                for k in range(3):
                    lcopy(g, layer, 1 + k, dev(x=xs[k])).start()
            g = t - LX
            if 0 <= g < GRP:
                exchange(g)
            g = t - LE
            if 0 <= g < GRP:
                exchanged(g)
                recon(g, sends)
                error_block(g, sends)
            for n in range(4):
                g = t - LE - GL * (n + 1)
                if 0 <= g < GRP:
                    gather_errors(g, n, sends)
        gathered()
        grads()
        recon_out()
        line_sums(GN - GLAG)

        def drain(i, _):
            for way in range(2):

                @pl.when(more[way])
                def _():
                    fcopy(h, i, way, nxt[way]).wait_send()

                    @pl.when(crosses0(i))
                    def _():
                        fcopy(1 - h, i, way, nxt[way]).wait_send()

                @pl.when(jnp.logical_not(crosses0(i)))
                def _():
                    fcopy(h, i, way, cross, fcs).wait_send()

            return 0

        lax.fori_loop(0, STEPS, drain, 0)
        for cp in xin:
            cp.wait_send()
        for cp in sends:
            cp.wait_send()
        grads_drain()

    def lcopy(g, m, n, to):
        r = RL[g].at[m]
        return copy(r, r, ls.at[g, n], lr.at[g, m], to)

    def lwait(g, m):
        arrived(RL[g].at[m], lr.at[g, m])

    def exchange(g):
        pair = 2 * x + 1 - h
        if g in ZG:

            @pl.when(x > 0)
            def _():
                lwait(g, pair)
                for k in range(3):
                    lcopy(g, pair, 4 + k, dev(x=xs[k])).start()

        else:
            for k in (0, 2, 1):

                @pl.when(xs[k] > 0)
                def _():
                    m = 2 * xs[k] + h
                    lwait(g, m)
                    lcopy(g, m, 4 + k, cross).start()

    def exchanged(g):
        for k in range(3):

            @pl.when(xs[k] > 0)
            def _():
                lwait(g, 2 * xs[k] + 1 - h)
                if g in ZG:
                    lwait(g, 2 * xs[k] + h)

        if g not in ZG:

            @pl.when(x > 0)
            def _():
                lwait(g, 2 * x + 1 - h)

    def exchange_drain():
        @pl.when(x > 0)
        def _():
            for g in range(GRP):
                lcopy(g, layer, 0, cross).wait_send()
                for k in range(3):
                    lcopy(g, layer, 1 + k, dev(x=xs[k])).wait_send()
            for g in ZG:
                for k in range(3):
                    lcopy(g, 2 * x + 1 - h, 4 + k, dev(x=xs[k])).wait_send()

        for g in range(GRP):
            if g in ZG:
                continue
            for k in range(3):

                @pl.when(xs[k] > 0)
                def _():
                    lcopy(g, 2 * xs[k] + h, 4 + k, cross).wait_send()

    place = []
    for p in range(6):
        at = jnp.int32(2)
        for i in range(6):
            at = jnp.where(dm[i] == p, jnp.int32(i + 2), at)
        place.append(at)

    def target_of(m):
        pair = dm[jnp.maximum(m - 2, 0)]
        return jnp.where(pair >= 3, pair - 2, pair)

    def recon(g, sends):
        for t in range(4):
            v = RL[g][place[PAIRS[t][0]]].astype(F32)
            for q in PAIRS[t][1:]:
                v = v + RL[g][place[q]].astype(F32)
            E[g, t] = v
        rcopy(E.at[g, :, other, :], ER.at[g], es.at[g], er.at[g], sib, sends)

    def recon_out():
        for g in range(GRP):
            arrived(ER.at[g], er.at[g])
            for cc in range(2):
                cols = slice(cc * HALF + GW * g, cc * HALF + GW * (g + 1))
                RO[:, :, cols] = jnp.where(c == cc, E[g, :, own, :], ER[g])
        pltpu.make_async_copy(RO, rec_out, osem.at[0]).start()

    def gcopy(n, k):
        to = xs[k]
        return copy(GS.at[n, pl.ds(2 * to, 2)], GA.at[n, x], gs.at[n, k], gr.at[n, x], dev(x=to))

    def zcopy(n):
        return copy(GC_.at[n], GZ.at[n], gzs.at[n], gzr.at[n], cross)

    def line_sum(n):
        for k in range(3):

            @pl.when(xs[k] > 0)
            def _():
                arrived(GA.at[n, xs[k]], gr.at[n, xs[k]])

        for s in range(2):
            mine, far = None, None
            for a in range(1, 4):
                on = (dm[2 * a + h - 2] >= 3) == (s == 1)
                p = jnp.where(on, GA[n, a, h].astype(F32), 0.0)
                q = jnp.where(on, GA[n, a, 1 - h].astype(F32), 0.0)
                mine = p if mine is None else mine + p
                far = q if far is None else far + q
            GO[n, s] = mine
            GC_[n, s] = far.astype(BF16)
        zcopy(n).start()

    def grads():
        def chunk(n, _):
            rows = pl.ds(pl.multiple_of(n * GC, GC), GC)
            GS[n] = against(None, rows).astype(BF16).reshape(8, ROWS, GC)
            for k in (0, 2, 1):
                gcopy(n, k).start()
            GA[n, x] = GS[n, pl.ds(2 * x, 2)]

            @pl.when(n >= GLAG)
            def _():
                line_sum(n - GLAG)

            return 0

        lax.fori_loop(0, GN, chunk, 0)

    def line_sums(start):
        def one(n, _):
            line_sum(n)
            return 0

        lax.fori_loop(start, GN, one, 0)

    def grads_drain():
        def drain(n, _):
            for k in range(3):
                gcopy(n, k).wait_send()
            return 0

        lax.fori_loop(0, GN, drain, 0)

    def grads_out():
        rows = pl.ds(pl.multiple_of(ROWS * layer, 8), ROWS)
        for n in range(GN):
            cols = slice(GC * n, GC * (n + 1))
            arrived(GZ.at[n], gzr.at[n])
            for s in range(2):
                v = GO[n, s] + GZ[n, s].astype(F32)
                on = gate_of(jnp.concatenate([TK[s, rows, :]] * (GC // 128), axis=1), FC[s : s + 1, cols])
                pg_out[s, :, cols] = jnp.where(on, v, 0.0).astype(BF16)
        for n in range(GN):
            zcopy(n).wait_send()

    def error_block(g, sends):
        cols = slice(GW * g, GW * (g + 1))
        for dst, t in ((X.at[c, g, l, y], target_of(layer)), (XO.at[g], target_of(2 * x + 1 - h))):
            dst[...] = (E[g, t] - tg[t, :, cols]).astype(BF16)
        errors_first(g, sends)

    def encoder_rest():
        sends = []
        for g in range(GRP + 2):
            if g < GRP:
                exchange(g)
            if g >= 2:
                exchanged(g - 2)
                recon(g - 2, sends)
        recon_out()
        line_sums(0)
        for cp in sends:
            cp.wait_send()

    enter()
    pl.when(x == 0)(encode)
    pl.when(x > 0)(decode)
    pl.when(x == 0)(encoder_rest)
    grads_out()
    exchange_drain()
    pltpu.make_async_copy(RO, rec_out, osem.at[0]).wait()


def body(sources, targets, blocks, enc_bias, token_code, feature_threshold_code, dec_map):
    vm = pl.BlockSpec(memory_space=pltpu.VMEM)
    V = pltpu.VMEM
    D = pltpu.SemaphoreType.DMA
    recon, pre_grads = pl.pallas_call(
        kernel,
        out_shape=(
            jax.ShapeDtypeStruct((4, 24, 4608), F32),
            jax.ShapeDtypeStruct((2, 48, 2048), BF16),
        ),
        in_specs=[pl.BlockSpec(memory_space=pltpu.SMEM), vm, vm, pl.BlockSpec(memory_space=pl.ANY), vm, vm, vm],
        out_specs=(pl.BlockSpec(memory_space=pl.ANY), vm),
        scratch_shapes=[
            V((2048, 4608), BF16),
            V((2, GRP, 2, 4, ROWS, GW), BF16),
            V((GRP, ROWS, GW), BF16),
            V((2, 2, NCH, 2, SUB, CH), BF16),
            V((2, 2, 192, HALF), F32),
            V((2, 24, HALF), F32),
            V((2, ROWS, HALF), F32),
            V((4, 24, HALF), F32),
            V((4, ROWS, HALF), F32),
            V((2, 384, 128), F32),
            V((2, 2048), F32),
            V((2, GRP, 4, ROWS, GW), BF16),
            V((2, GRP, 4, ROWS, GW), BF16),
            V((2, GRP, 4, ROWS, GW), BF16),
            V((2, GRP, 3, ROWS, GW), BF16),
            V((GRP, ROWS, GW), BF16),
            V((GRP, ROWS, GW), BF16),
            V((8, ROWS, GW), BF16),
            V((8, ROWS, GW), BF16),
            V((8, ROWS, GW), BF16),
            V((8, ROWS, GW), BF16),
            V((8, ROWS, GW), BF16),
            V((8, ROWS, GW), BF16),
            V((GRP, 4, ROWS, GW), F32),
            V((GRP, 4, 24, GW), F32),
            V((4, 24, 4608), F32),
            V((GN, 8, ROWS, GC), BF16),
            V((GN, 4, 2, ROWS, GC), BF16),
            V((GN, 2, ROWS, GC), F32),
            V((GN, 2, ROWS, GC), BF16),
            V((GN, 2, ROWS, GC), BF16),
            D((NCH,)),
            D((4,)),
            D((128,)),
            D((GRP, 2, 4, 2)),
            D((GRP, 2, 4)),
            D((2, 2, NCH, 2)),
            D((2, 2, NCH, 2)),
            D((2, 2, NCH, 2)),
            D((2, GRP)),
            D((2, GRP)),
            D((2, GRP, 3)),
            D((2, GRP, 3)),
            D((GRP,)),
            D((GRP,)),
            D((GRP, 7)),
            D((GRP, 8)),
            D((GRP,)),
            D((GRP,)),
            D((GN, 3)),
            D((GN, 4)),
            D((GN,)),
            D((GN,)),
            D((1,)),
        ],
        compiler_params=pltpu.CompilerParams(
            collective_id=1, has_side_effects=True, vmem_limit_bytes=62 * 2**20
        ),
        name="transcoder",
    )(dec_map, sources, targets, blocks, enc_bias, token_code, feature_threshold_code)
    return recon - targets.astype(F32), pre_grads


def solution(mesh):
    return jax.shard_map(
        body,
        mesh=mesh,
        in_specs=(
            P(None, "feat", None),
            P(None, "feat", None),
            P("layer", "feat", None),
            P(None, "feat"),
            P(),
            P(None, "feat"),
            P(),
        ),
        out_specs=(P(None, "feat", None), P(None, "layer", "feat")),
        check_vma=False,
    )
```

```python
import jax
import jax.numpy as jnp
from jax import lax
from jax.experimental import pallas as pl
from jax.experimental.pallas import tpu as pltpu
from jax.sharding import PartitionSpec as P

MESH = pl.DeviceIdType.MESH
F32 = jnp.float32
BF16 = jnp.bfloat16

ROWS = 48
HALF = 2304
GRP = 6
GW = 384
DW = 768
NCH = 8
CH = 256
SUB = 96
STEPS = 2 * NCH
CROSS0 = 3
FLAG = 5
LH = 3
ML = 12
GN = 8
GC = 256
GLAG = 3
ZG = (3, 4, 5)
LC = 2
LX = 5
LE = 9
GL = 3

NT = (((1,), (1,)), ((), ()))
PAIRS = ((0,), (1, 3), (2, 4), (5,))


def gate_of(tok, code):
    v = tok * code
    q = jnp.floor(v * (1.0 / 251.0))
    return (v - 251.0 * q) < 40.0


def kernel(
    dm, src, tgt, w_hbm, bias, tok, fc, rec_out, pg_out,
    W, X, XO, FB, acc, sx_send, sx, tg_send, tg, TK, FC,
    S, C, T, RY, V1, RZ, R0, R1, R2, R3, R4, R5, E, ER, RO, GS, GA, GO, GC_, GZ,
    wsem, xsem, ags, agr, br, fs, fcs, fr, ss, sr, ys_s, ys_r, zs, zr, ls, lr, es, er, gs, gr, gzs, gzr, osem,
):
    layer = lax.axis_index("layer")
    feat = lax.axis_index("feat")
    x, h = layer // 2, layer % 2
    l, y, c = feat // 8, (feat // 2) % 4, feat % 2
    o = 1 - c
    RL = (R0, R1, R2, R3, R4, R5)

    def dev(x=x, h=h, l=l, y=y, c=c):
        return (2 * x + h, (4 * l + y) * 2 + c)

    ys = [lax.rem(y + k, 4) for k in (1, 2, 3)]
    xs = [lax.rem(x + k, 4) for k in (1, 2, 3)]
    sib = dev(c=o)
    zp = dev(l=1 - l)
    zo = dev(h=1 - h, l=1 - l)
    cross = dev(h=1 - h)

    def copy(a, b, ssem, rsem, to):
        return pltpu.make_async_remote_copy(
            src_ref=a, dst_ref=b, send_sem=ssem, recv_sem=rsem, device_id=to, device_id_type=MESH
        )

    def rcopy(a, b, ssem, rsem, to, sends):
        cp = copy(a, b, ssem, rsem, to)
        cp.start()
        sends.append(cp)

    def arrived(b, rsem):
        copy(b, b, rsem, rsem, sib).wait_recv()

    def half_of(v, which):
        return jnp.where(which == 0, v[..., :HALF], v[..., HALF:])

    own = pl.ds(pl.multiple_of(24 * c, 8), 24)
    other = pl.ds(pl.multiple_of(24 * o, 8), 24)

    def enter():
        bar = pltpu.get_barrier_semaphore()
        peers = [sib, zp, zo, cross] + [dev(y=a) for a in ys]
        peers += [dev(x=a) for a in xs] + [dev(x=a, h=1 - h) for a in xs]
        for p in peers:
            pl.semaphore_signal(bar, inc=1, device_id=p, device_id_type=MESH)
        for k in range(NCH):
            rows = pl.ds(CH * k, CH)
            pltpu.make_async_copy(w_hbm.at[0, rows], W.at[rows], wsem.at[k]).start()
        v = src[...].astype(F32)
        sx_send[...] = half_of(v, o)
        sx[:, own, :] = half_of(v, c)
        codes()
        pl.semaphore_wait(bar, len(peers))

    def sources_in(sends):
        rcopy(sx_send, sx.at[:, own, :], xsem.at[0], xsem.at[1], sib, sends)
        arrived(sx.at[:, other, :], xsem.at[1])

    def targets_out(sends):
        for t in range(4):
            v = tgt[t].astype(F32)
            tg_send[t] = half_of(v, o)
            tg[t, own, :] = half_of(v, c)
        rcopy(tg_send, tg.at[:, own, :], xsem.at[2], xsem.at[3], sib, sends)

    def codes():
        for s in range(2):
            TK[s] = jnp.transpose(jnp.broadcast_to(tok[s : s + 1, :].astype(F32), (128, 384)))
        FC[...] = fc[...].astype(F32)

    yp, y2, ym = ys

    def parts(g):
        m = 128 if g % 2 == 0 else 256
        return pl.ds(0, m), pl.ds(m, GW - m)

    count = [0]

    def gsend(src_ref, at, cols, to, rsem, sends):
        dst = X.at[at] if cols is None else X.at[at + (slice(None), cols)]
        a = src_ref if cols is None else src_ref.at[:, cols]
        rcopy(a, dst, ags.at[count[0]], rsem, to, sends)
        count[0] += 1

    def rsem_of(g, ll, yy, part=0):
        return agr.at[g, ll, yy, part]

    def both(g, ll, yy, sends):
        at = (c, g, ll, yy)
        gsend(X.at[at], at, None, sib, br.at[g, ll, yy], sends)

    def gather_first(g, sends):
        at = (c, g, l, y)
        r = X.at[at]
        for to in (yp, ym):
            gsend(r, at, None, dev(y=to), rsem_of(g, l, y), sends)
        if g % 2 == 0:
            gsend(XO.at[g], at, None, zo, rsem_of(g, l, y), sends)
        else:
            gsend(r, at, None, zp, rsem_of(g, l, y), sends)
        both(g, l, y, sends)

    def gather_own(sends):
        for g in range(GRP):
            lo, hi = parts(g)
            for frm, to, cols, part in ((ym, yp, lo, 0), (yp, ym, hi, 1)):
                at = (c, g, l, frm)
                arrived(X.at[at], rsem_of(g, l, frm))
                gsend(X.at[at], at, cols, dev(y=to), rsem_of(g, l, frm, part), sends)
                both(g, l, frm, sends)
        for g in range(GRP):
            at = (c, g, 1 - l, y)
            arrived(X.at[at], rsem_of(g, 1 - l, y))
            for to in (yp, ym, y2):
                gsend(X.at[at], at, None, dev(y=to), rsem_of(g, 1 - l, y), sends)
            both(g, 1 - l, y, sends)
        for g in range(GRP):
            lo, hi = parts(g)
            arrived(X.at[c, g, l, y2, :, lo], rsem_of(g, l, y2, 0))
            arrived(X.at[c, g, l, y2, :, hi], rsem_of(g, l, y2, 1))
            both(g, l, y2, sends)
        for g in range(GRP):
            for yy in range(4):
                arrived(X.at[o, g, l, yy], br.at[g, l, yy])

    def gather_rest(sends):
        for g in range(GRP):
            for frm in (ym, yp, y2):
                arrived(X.at[c, g, 1 - l, frm], rsem_of(g, 1 - l, frm))
                both(g, 1 - l, frm, sends)
        for g in range(GRP):
            for yy in range(4):
                arrived(X.at[o, g, 1 - l, yy], br.at[g, 1 - l, yy])

    def errors_first(g, sends):
        at = (c, g, l, y)
        r = X.at[at]
        gsend(XO.at[g], at, None, zo, rsem_of(g, l, y), sends)
        for to in (yp, ym):
            gsend(r, at, None, dev(y=to), rsem_of(g, l, y), sends)
        both(g, l, y, sends)

    def from_y(g, ll, sends, on_z):
        lo, hi = parts(g)
        for frm, to, cols, part in ((ym, yp, lo, 0), (yp, ym, hi, 1)):
            at = (c, g, ll, frm)
            arrived(X.at[at], rsem_of(g, ll, frm))
            gsend(X.at[at], at, cols, dev(y=to), rsem_of(g, ll, frm, part), sends)
            if on_z:
                gsend(X.at[at], at, None, zp, rsem_of(g, ll, frm), sends)
            both(g, ll, frm, sends)

    def from_y2(g, ll, sends, on_z):
        lo, hi = parts(g)
        at = (c, g, ll, y2)
        arrived(X.at[at + (slice(None), lo)], rsem_of(g, ll, y2, 0))
        arrived(X.at[at + (slice(None), hi)], rsem_of(g, ll, y2, 1))
        if on_z:
            gsend(X.at[at], at, None, zp, rsem_of(g, ll, y2), sends)
        both(g, ll, y2, sends)

    def from_z(g, yy, sends, on_y):
        at = (c, g, 1 - l, yy)
        arrived(X.at[at], rsem_of(g, 1 - l, yy))
        if on_y:
            for to in (yp, ym):
                gsend(X.at[at], at, None, dev(y=to), rsem_of(g, 1 - l, yy), sends)
        both(g, 1 - l, yy, sends)

    def gather_errors(g, n, sends):
        if g in ZG:
            if n == 0:
                from_z(g, y, sends, True)
                from_y(g, l, sends, False)
            elif n == 1:
                from_y(g, 1 - l, sends, False)
                from_y2(g, l, sends, False)
            elif n == 2:
                from_y2(g, 1 - l, sends, False)
        elif n == 0:
            from_y(g, l, sends, True)
        elif n == 1:
            from_y2(g, l, sends, True)
            from_z(g, y, sends, False)
        elif n == 2:
            from_z(g, ym, sends, False)
            from_z(g, yp, sends, False)
        else:
            from_z(g, y2, sends, False)

    def gathered():
        for g in range(GRP):
            for ll in range(2):
                for yy in range(4):
                    arrived(X.at[o, g, ll, yy], br.at[g, ll, yy])

    def against(lh, rows):
        total = None
        for cc in range(2):
            for n in range(HALF // DW):
                a = [X[cc, g] if lh is None else X[cc, g, lh] for g in (2 * n, 2 * n + 1)]
                a = jnp.concatenate([v.reshape(-1, GW) for v in a], axis=1)
                b = W[rows, cc * HALF + n * DW : cc * HALF + (n + 1) * DW]
                d = lax.dot_general(a, b, NT, preferred_element_type=F32)
                total = d if total is None else total + d
        return total

    def piece(s, i):
        return s, lax.rem(l + i // NCH, 2), lax.rem(i, NCH)

    def fcopy(s, i, way, to, sem=None):
        s, lh, k = piece(s, i)
        r = FB.at[s, lh, k, way]
        return copy(r, r, (fs if sem is None else sem).at[s, lh, k, way], fr.at[s, lh, k, way], to)

    def farrived(s, i, way):
        s, lh, k = piece(s, i)
        arrived(FB.at[s, lh, k, way], fr.at[s, lh, k, way])

    def crosses0(i):
        return lax.rem(i, NCH) < CROSS0

    def encode():
        sends = []
        sources_in(sends)
        for g in range(GRP):
            cols = slice(GW * g, GW * (g + 1))
            X[c, g, l, y] = sx[h, :, cols].astype(BF16)
            XO[g] = sx[1 - h, :, cols].astype(BF16)
            gather_first(g, sends)
        gather_own(sends)
        line = (dev(x=1), dev(x=3))

        def chunk(i, _):
            _, lh, k = piece(h, i)
            rows = pl.ds(pl.multiple_of(k * CH, CH), CH)

            @pl.when(i < NCH)
            def _():
                pltpu.make_async_copy(w_hbm.at[0, rows], W.at[rows], wsem.at[k]).wait()

            pre = against(lh, rows) + bias[pl.ds(h, 1), rows]
            toks = TK[h, pl.ds(pl.multiple_of(lh * 192, 8), 192), :]
            on = gate_of(jnp.concatenate([toks] * 2, axis=1), FC[pl.ds(h, 1), rows])
            FB[h, lh, k] = jnp.where(on, pre, 0.0).astype(BF16).reshape(2, SUB, CH)
            for way in range(2):
                fcopy(h, i, way, line[way]).start()

            @pl.when(crosses0(i))
            def _():
                for way in range(2):
                    fcopy(h, i, way, cross, fcs).start()

            j = i - FLAG

            @pl.when((j >= 0) & crosses0(j + NCH))
            def _():
                for way in range(2):
                    farrived(1 - h, j, way)
                    fcopy(1 - h, j, way, line[way]).start()

            return 0

        lax.fori_loop(0, NCH, chunk, 0)
        targets_out(sends)
        gather_rest(sends)
        lax.fori_loop(NCH, STEPS, chunk, 0)

        def drain(i, _):
            for way in range(2):
                fcopy(h, i, way, line[way]).wait_send()

                @pl.when(crosses0(i))
                def _():
                    fcopy(h, i, way, cross, fcs).wait_send()
                    fcopy(1 - h, i, way, line[way]).wait_send()

            return 0

        lax.fori_loop(0, STEPS, drain, 0)
        for cp in sends:
            cp.wait_send()
        arrived(tg.at[:, other, :], xsem.at[3])

    def lh_of(j):
        return l if j == 0 else 1 - l

    def fold_start(j, sends):
        for g in range(GRP):
            cols = slice(GW * g, GW * (g + 1))
            S[j, g] = acc[o, lh_of(j), :, cols].astype(BF16).reshape(4, ROWS, GW)
            rcopy(S.at[j, g], C.at[j, g], ss.at[j, g], sr.at[j, g], sib, sends)

    def fold_end(j, sends):
        for g in range(GRP):
            cols = slice(GW * g, GW * (g + 1))
            arrived(C.at[j, g], sr.at[j, g])
            v = acc[c, lh_of(j), :, cols] + C[j, g].astype(F32).reshape(192, GW)
            T[j, g] = v.astype(BF16).reshape(4, ROWS, GW)
            for k in (0, 2, 1):
                rcopy(T.at[j, g, ys[k]], RY.at[j, g, 2 - k], ys_s.at[j, g, k], ys_r.at[j, g, 2 - k], dev(y=ys[k]), sends)

    def fold_sum(j, g):
        for k in range(3):
            arrived(RY.at[j, g, k], ys_r.at[j, g, k])
        v = T[j, g, y].astype(F32)
        for k in range(3):
            v = v + RY[j, g, k].astype(F32)
        return v

    def decode():
        sends = []
        acc[...] = jnp.zeros_like(acc)
        xin = []
        sources_in(xin)
        targets_out(xin)
        nxt = (dev(x=lax.rem(x + 1, 4)), dev(x=lax.rem(x + 3, 4)))
        more = (x < 3, x > 1)
        lag = ((x - 1) * LH, (3 - x) * LH)
        mine_src = (dm[layer - 2] >= 3).astype(jnp.int32)

        def step(t, _):
            for way in range(2):
                i = t - lag[way]

                @pl.when((i >= 0) & (i < STEPS))
                def _():
                    farrived(h, i, way)

                    @pl.when(more[way])
                    def _():
                        fcopy(h, i, way, nxt[way]).start()

                    @pl.when(jnp.logical_not(crosses0(i)))
                    def _():
                        fcopy(h, i, way, cross, fcs).start()

                j = i - FLAG

                @pl.when((j >= 0) & (j < STEPS) & crosses0(j + 2 * NCH))
                def _():
                    farrived(1 - h, j, way)

                    @pl.when(more[way])
                    def _():
                        fcopy(1 - h, j, way, nxt[way]).start()

            m = t - ML

            @pl.when(m >= 0)
            def _():
                @pl.when(jnp.logical_not(crosses0(m)))
                def _():
                    for way in range(2):
                        farrived(1 - h, m, way)

                _, lh, k = piece(h, m)
                rows = pl.ds(pl.multiple_of(k * CH, CH), CH)

                @pl.when(m < NCH)
                def _():
                    pltpu.make_async_copy(w_hbm.at[0, rows], W.at[rows], wsem.at[k]).wait()

                a = jnp.where(mine_src == 0, FB[0, lh, k], FB[1, lh, k]).reshape(192, CH)
                for cc in range(2):
                    for n in range(HALF // DW):
                        cols = slice(cc * HALF + n * DW, cc * HALF + (n + 1) * DW)
                        acc[cc, lh, :, n * DW : (n + 1) * DW] += jnp.dot(a, W[rows, cols], preferred_element_type=F32)

            return 0

        lax.fori_loop(0, NCH + ML, step, 0)
        fold_start(0, sends)
        lax.fori_loop(NCH + ML, NCH + ML + 2, step, 0)
        fold_end(0, sends)
        lax.fori_loop(NCH + ML + 2, STEPS + ML, step, 0)
        fold_start(1, sends)
        fold_end(1, sends)

        arrived(tg.at[:, other, :], xsem.at[3])
        count[0] = 0
        for t in range(GRP + LE + 4 * GL):
            g = t
            if g < GRP:
                V1[g] = fold_sum(1, g).astype(BF16)
                rcopy(V1.at[g], RZ.at[g], zs.at[g], zr.at[g], zp, sends)
            g = t - LC
            if 0 <= g < GRP:
                v = fold_sum(0, g)
                arrived(RZ.at[g], zr.at[g])
                RL[g][layer] = (v + RZ[g].astype(F32)).astype(BF16)
                lcopy(g, layer, 0, cross).start()
                for k in range(3):
                    lcopy(g, layer, 1 + k, dev(x=xs[k])).start()
            g = t - LX
            if 0 <= g < GRP:
                exchange(g)
            g = t - LE
            if 0 <= g < GRP:
                exchanged(g)
                recon(g, sends)
                error_block(g, sends)
            for n in range(4):
                g = t - LE - GL * (n + 1)
                if 0 <= g < GRP:
                    gather_errors(g, n, sends)
        gathered()
        grads()
        recon_out()
        line_sums(GN - GLAG)

        def drain(i, _):
            for way in range(2):

                @pl.when(more[way])
                def _():
                    fcopy(h, i, way, nxt[way]).wait_send()

                    @pl.when(crosses0(i))
                    def _():
                        fcopy(1 - h, i, way, nxt[way]).wait_send()

                @pl.when(jnp.logical_not(crosses0(i)))
                def _():
                    fcopy(h, i, way, cross, fcs).wait_send()

            return 0

        lax.fori_loop(0, STEPS, drain, 0)
        for cp in xin:
            cp.wait_send()
        for cp in sends:
            cp.wait_send()
        grads_drain()

    def lcopy(g, m, n, to):
        r = RL[g].at[m]
        return copy(r, r, ls.at[g, n], lr.at[g, m], to)

    def lwait(g, m):
        arrived(RL[g].at[m], lr.at[g, m])

    def exchange(g):
        pair = 2 * x + 1 - h
        if g in ZG:

            @pl.when(x > 0)
            def _():
                lwait(g, pair)
                for k in range(3):
                    lcopy(g, pair, 4 + k, dev(x=xs[k])).start()

        else:
            for k in (0, 2, 1):

                @pl.when(xs[k] > 0)
                def _():
                    m = 2 * xs[k] + h
                    lwait(g, m)
                    lcopy(g, m, 4 + k, cross).start()

    def exchanged(g):
        for k in range(3):

            @pl.when(xs[k] > 0)
            def _():
                lwait(g, 2 * xs[k] + 1 - h)
                if g in ZG:
                    lwait(g, 2 * xs[k] + h)

        if g not in ZG:

            @pl.when(x > 0)
            def _():
                lwait(g, 2 * x + 1 - h)

    def exchange_drain():
        @pl.when(x > 0)
        def _():
            for g in range(GRP):
                lcopy(g, layer, 0, cross).wait_send()
                for k in range(3):
                    lcopy(g, layer, 1 + k, dev(x=xs[k])).wait_send()
            for g in ZG:
                for k in range(3):
                    lcopy(g, 2 * x + 1 - h, 4 + k, dev(x=xs[k])).wait_send()

        for g in range(GRP):
            if g in ZG:
                continue
            for k in range(3):

                @pl.when(xs[k] > 0)
                def _():
                    lcopy(g, 2 * xs[k] + h, 4 + k, cross).wait_send()

    place = []
    for p in range(6):
        at = jnp.int32(2)
        for i in range(6):
            at = jnp.where(dm[i] == p, jnp.int32(i + 2), at)
        place.append(at)

    def target_of(m):
        pair = dm[jnp.maximum(m - 2, 0)]
        return jnp.where(pair >= 3, pair - 2, pair)

    def recon(g, sends):
        for t in range(4):
            v = RL[g][place[PAIRS[t][0]]].astype(F32)
            for q in PAIRS[t][1:]:
                v = v + RL[g][place[q]].astype(F32)
            E[g, t] = v
        rcopy(E.at[g, :, other, :], ER.at[g], es.at[g], er.at[g], sib, sends)

    def recon_out():
        for g in range(GRP):
            arrived(ER.at[g], er.at[g])
            for cc in range(2):
                cols = slice(cc * HALF + GW * g, cc * HALF + GW * (g + 1))
                RO[:, :, cols] = jnp.where(c == cc, E[g, :, own, :], ER[g])
        pltpu.make_async_copy(RO, rec_out, osem.at[0]).start()

    def gcopy(n, k):
        to = xs[k]
        return copy(GS.at[n, pl.ds(2 * to, 2)], GA.at[n, x], gs.at[n, k], gr.at[n, x], dev(x=to))

    def zcopy(n):
        return copy(GC_.at[n], GZ.at[n], gzs.at[n], gzr.at[n], cross)

    def line_sum(n):
        for k in range(3):

            @pl.when(xs[k] > 0)
            def _():
                arrived(GA.at[n, xs[k]], gr.at[n, xs[k]])

        for s in range(2):
            mine, far = None, None
            for a in range(1, 4):
                on = (dm[2 * a + h - 2] >= 3) == (s == 1)
                p = jnp.where(on, GA[n, a, h].astype(F32), 0.0)
                q = jnp.where(on, GA[n, a, 1 - h].astype(F32), 0.0)
                mine = p if mine is None else mine + p
                far = q if far is None else far + q
            GO[n, s] = mine
            GC_[n, s] = far.astype(BF16)
        zcopy(n).start()

    def grads():
        def chunk(n, _):
            rows = pl.ds(pl.multiple_of(n * GC, GC), GC)
            GS[n] = against(None, rows).astype(BF16).reshape(8, ROWS, GC)
            for k in (0, 2, 1):
                gcopy(n, k).start()
            GA[n, x] = GS[n, pl.ds(2 * x, 2)]

            @pl.when(n >= GLAG)
            def _():
                line_sum(n - GLAG)

            return 0

        lax.fori_loop(0, GN, chunk, 0)

    def line_sums(start):
        def one(n, _):
            line_sum(n)
            return 0

        lax.fori_loop(start, GN, one, 0)

    def grads_drain():
        def drain(n, _):
            for k in range(3):
                gcopy(n, k).wait_send()
            return 0

        lax.fori_loop(0, GN, drain, 0)

    def grads_out():
        rows = pl.ds(pl.multiple_of(ROWS * layer, 8), ROWS)
        for n in range(GN):
            cols = slice(GC * n, GC * (n + 1))
            arrived(GZ.at[n], gzr.at[n])
            for s in range(2):
                v = GO[n, s] + GZ[n, s].astype(F32)
                on = gate_of(jnp.concatenate([TK[s, rows, :]] * (GC // 128), axis=1), FC[s : s + 1, cols])
                pg_out[s, :, cols] = jnp.where(on, v, 0.0).astype(BF16)
        for n in range(GN):
            zcopy(n).wait_send()

    def error_block(g, sends):
        cols = slice(GW * g, GW * (g + 1))
        for dst, t in ((X.at[c, g, l, y], target_of(layer)), (XO.at[g], target_of(2 * x + 1 - h))):
            dst[...] = (E[g, t] - tg[t, :, cols]).astype(BF16)
        errors_first(g, sends)

    def encoder_rest():
        sends = []
        for g in range(GRP + 2):
            if g < GRP:
                exchange(g)
            if g >= 2:
                exchanged(g - 2)
                recon(g - 2, sends)
        recon_out()
        line_sums(0)
        for cp in sends:
            cp.wait_send()

    enter()
    pl.when(x == 0)(encode)
    pl.when(x > 0)(decode)
    pl.when(x == 0)(encoder_rest)
    grads_out()
    exchange_drain()
    pltpu.make_async_copy(RO, rec_out, osem.at[0]).wait()


def body(sources, targets, blocks, enc_bias, token_code, feature_threshold_code, dec_map):
    vm = pl.BlockSpec(memory_space=pltpu.VMEM)
    V = pltpu.VMEM
    D = pltpu.SemaphoreType.DMA
    recon, pre_grads = pl.pallas_call(
        kernel,
        out_shape=(
            jax.ShapeDtypeStruct((4, 24, 4608), F32),
            jax.ShapeDtypeStruct((2, 48, 2048), BF16),
        ),
        in_specs=[pl.BlockSpec(memory_space=pltpu.SMEM), vm, vm, pl.BlockSpec(memory_space=pl.ANY), vm, vm, vm],
        out_specs=(pl.BlockSpec(memory_space=pl.ANY), vm),
        scratch_shapes=[
            V((2048, 4608), BF16),
            V((2, GRP, 2, 4, ROWS, GW), BF16),
            V((GRP, ROWS, GW), BF16),
            V((2, 2, NCH, 2, SUB, CH), BF16),
            V((2, 2, 192, HALF), F32),
            V((2, 24, HALF), F32),
            V((2, ROWS, HALF), F32),
            V((4, 24, HALF), F32),
            V((4, ROWS, HALF), F32),
            V((2, 384, 128), F32),
            V((2, 2048), F32),
            V((2, GRP, 4, ROWS, GW), BF16),
            V((2, GRP, 4, ROWS, GW), BF16),
            V((2, GRP, 4, ROWS, GW), BF16),
            V((2, GRP, 3, ROWS, GW), BF16),
            V((GRP, ROWS, GW), BF16),
            V((GRP, ROWS, GW), BF16),
            V((8, ROWS, GW), BF16),
            V((8, ROWS, GW), BF16),
            V((8, ROWS, GW), BF16),
            V((8, ROWS, GW), BF16),
            V((8, ROWS, GW), BF16),
            V((8, ROWS, GW), BF16),
            V((GRP, 4, ROWS, GW), F32),
            V((GRP, 4, 24, GW), F32),
            V((4, 24, 4608), F32),
            V((GN, 8, ROWS, GC), BF16),
            V((GN, 4, 2, ROWS, GC), BF16),
            V((GN, 2, ROWS, GC), F32),
            V((GN, 2, ROWS, GC), BF16),
            V((GN, 2, ROWS, GC), BF16),
            D((NCH,)),
            D((4,)),
            D((128,)),
            D((GRP, 2, 4, 2)),
            D((GRP, 2, 4)),
            D((2, 2, NCH, 2)),
            D((2, 2, NCH, 2)),
            D((2, 2, NCH, 2)),
            D((2, GRP)),
            D((2, GRP)),
            D((2, GRP, 3)),
            D((2, GRP, 3)),
            D((GRP,)),
            D((GRP,)),
            D((GRP, 7)),
            D((GRP, 8)),
            D((GRP,)),
            D((GRP,)),
            D((GN, 3)),
            D((GN, 4)),
            D((GN,)),
            D((GN,)),
            D((1,)),
        ],
        compiler_params=pltpu.CompilerParams(
            collective_id=1, has_side_effects=True, vmem_limit_bytes=62 * 2**20
        ),
        name="transcoder",
    )(dec_map, sources, targets, blocks, enc_bias, token_code, feature_threshold_code)
    return recon - targets.astype(F32), pre_grads


def solution(mesh):
    return jax.shard_map(
        body,
        mesh=mesh,
        in_specs=(
            P(None, "feat", None),
            P(None, "feat", None),
            P("layer", "feat", None),
            P(None, "feat"),
            P(),
            P(None, "feat"),
            P(),
        ),
        out_specs=(P(None, "feat", None), P(None, "layer", "feat")),
        check_vma=False,
    )
```
